128 devices in a mesh: grp: 8 (over y, core), slc: 16 (over x, z).
Axes of the slice: x: 4, y: 4, z: 4, core: 2. Of those that a mesh axis runs over, the one named last changes fastest.
Arguments:
- tokens: bfloat16 [16384, 4096], P(('grp', 'slc')), may hold values from -6 to 6
- expert_ids: int32 [16384, 8], P(('grp', 'slc')), may hold values from 0 to 127, as said below
- slot_positions: int32 [16384, 8], P(('grp', 'slc')), may hold values from 0 to 10, as said below
- gate_probs: float32 [16384, 8], P(('grp', 'slc')), may hold values from 0.1 to 0.5
- w_gate: bfloat16 [128, 4096, 768], P(('grp', 'slc')), may hold values from -0.09375 to 0.09375
- w_up: bfloat16 [128, 4096, 768], P(('grp', 'slc')), may hold values from -0.09375 to 0.09375
- w_down: bfloat16 [128, 768, 4096], P(('grp', 'slc')), may hold values from -0.21875 to 0.21875
Outputs:
- moe_out: bfloat16 [16384, 4096], P(('grp', 'slc'))
The draws below stay inside these ranges and needn't reach their ends.
Inputs may be any that keep to these rules, and one draw needn't show every extreme that they name: `expert_ids`: each token's 8 experts differ. Some expert is chosen by 10 or more tokens of every block of 128 tokens. `slot_positions`: within a block of 128 tokens, a choice's slot is the number of earlier choices of the block (tokens in order, then k in order) that name the same expert, or 10 where that number is 10 or more (the choice is dropped).
All inputs are finite; a program needn't handle non-finite values.
Results may differ from the reference program's by a relative error of at most 0.011.
Values may be sent and summed in bfloat16 or wider, within the bound.
A program may use at most 128 MiB of HBM per device.

```python
import jax
import jax.numpy as jnp
from jax import lax

D = 4096
H = 768
TOP = 8
TOK_DEV = 128
EXPERTS = 128
TOKENS = 16384
CAP_PAIR = 10


def route_tables(key):
    blocks = TOKENS // TOK_DEV
    hot_key = jax.random.fold_in(key, 11)
    offset_key = jax.random.fold_in(key, 12)
    score_key = jax.random.fold_in(key, 13)
    bias_key = jax.random.fold_in(key, 14)
    hot_expert = jax.random.randint(hot_key, (), 0, EXPERTS)
    offset = jax.random.randint(offset_key, (blocks, 1), 0, TOK_DEV)
    local = jnp.arange(TOK_DEV, dtype=jnp.int32)[None, :]
    forced = (local + offset) % TOK_DEV < CAP_PAIR + TOK_DEV // 8
    expert_iota = jnp.arange(EXPERTS, dtype=jnp.int32)
    bias = jax.random.randint(bias_key, (EXPERTS,), 0, 32768)
    raw = jax.random.randint(score_key, (blocks, TOK_DEV, EXPERTS), 0, 32768) + bias
    is_hot = (expert_iota == hot_expert)[None, None, :]
    raw = jnp.where(is_hot & forced[:, :, None], 65536, raw)
    score = raw * EXPERTS + expert_iota
    chosen = lax.top_k(score, TOP)[1].astype(jnp.int32)
    flat = chosen.reshape(blocks, TOK_DEV * TOP)
    onehot = (flat[:, :, None] == expert_iota[None, None, :]).astype(jnp.int32)
    earlier = jnp.cumsum(onehot, axis=1) - onehot
    ranks = jnp.sum(earlier * onehot, axis=-1)
    slots = jnp.minimum(ranks, CAP_PAIR).astype(jnp.int32)
    return (chosen.reshape(TOKENS, TOP), slots.reshape(TOKENS, TOP))


def draw_expert_ids(key, part):
    chosen, slots = route_tables(key)
    return chosen


def draw_slot_positions(key, part):
    chosen, slots = route_tables(key)
    return slots


def levels(own_key, dims, shards, low, largest):
    def one(dim, blocks):
        draws = jax.random.uniform(jax.random.fold_in(jax.random.fold_in(own_key, 6), dim), (blocks,), jnp.float32, low / len(shards), largest / len(shards))
        return jnp.repeat(jnp.exp(draws), dims[dim] // blocks).reshape((-1,) + (1,) * (len(dims) - dim - 1))

    factor_of = one(*shards[0])
    for cut in shards[1:]:
        factor_of = factor_of * one(*cut)
    return factor_of


def bell_draw(stream_key, extent, spread, reach, shards=(), kind=jnp.bfloat16):
    array = spread * jax.random.normal(stream_key, extent, jnp.float32)
    if shards:
        array = array * levels(stream_key, extent, shards, -0.22, 0.18)
    return jnp.clip(array, -reach, reach).astype(kind)


def setup_inputs(seed: int = 0) -> dict:
    key_of = jax.random.split(jax.random.key(seed), 8)
    tokens = bell_draw(key_of[0], (TOKENS, D), 1.0, 6.0, ((0, 128),))
    expert_ids = draw_expert_ids(jax.random.fold_in(key_of[7], 71), 0)
    slot_positions = draw_slot_positions(jax.random.fold_in(key_of[7], 71), 0)
    gate_probs = jnp.clip(0.1 + 0.4 * jax.random.uniform(key_of[3], (TOKENS, TOP), jnp.float32) ** levels(key_of[3], (TOKENS, TOP), ((0, 128),), -0.2, 0.2), 0.1, 0.5)
    w_gate = bell_draw(key_of[4], (EXPERTS, D, H), D ** -0.5, 0.09375, ((0, 128),))
    w_up = bell_draw(key_of[5], (EXPERTS, D, H), D ** -0.5, 0.09375, ((0, 128),))
    w_down = bell_draw(key_of[6], (EXPERTS, H, D), H ** -0.5, 0.21875, ((0, 128),))
    return {"tokens": tokens, "expert_ids": expert_ids, "slot_positions": slot_positions, "gate_probs": gate_probs, "w_gate": w_gate, "w_up": w_up, "w_down": w_down}


def reference(tokens, expert_ids, slot_positions, gate_probs, w_gate, w_up, w_down):
    blocks = TOKENS // TOK_DEV
    token_index = jnp.arange(TOKENS, dtype=jnp.int32)
    block_index = token_index // TOK_DEV
    kept = slot_positions < CAP_PAIR
    target = (expert_ids * blocks + block_index[:, None]) * CAP_PAIR + jnp.minimum(slot_positions, CAP_PAIR - 1)
    dump = EXPERTS * blocks * CAP_PAIR
    target = jnp.where(kept, target, dump).astype(jnp.int32)
    sources = jnp.broadcast_to(token_index[:, None], target.shape).reshape(-1)
    table = jnp.full((dump + 1,), TOKENS, jnp.int32).at[target.reshape(-1)].set(sources)
    table = table[:dump].reshape(EXPERTS, blocks * CAP_PAIR)
    padded = jnp.concatenate([tokens, jnp.zeros((1, D), tokens.dtype)], 0)

    def run_expert(inputs):
        rows_index, gate_w, up_w, down_w = inputs
        rows = padded[rows_index]
        gate = jnp.dot(rows, gate_w, preferred_element_type=jnp.float32)
        up = jnp.dot(rows, up_w, preferred_element_type=jnp.float32)
        hidden = (jax.nn.silu(gate) * up).astype(jnp.bfloat16)
        return jnp.dot(hidden, down_w, preferred_element_type=jnp.float32).astype(jnp.bfloat16)

    outputs = lax.map(run_expert, (table, w_gate, w_up, w_down)).reshape(dump, D)
    total = jnp.zeros((TOKENS, D), jnp.float32)
    for choice_index in range(TOP):
        picked = outputs[jnp.minimum(target[:, choice_index], dump - 1)].astype(jnp.float32)
        weight = jnp.where(kept[:, choice_index], gate_probs[:, choice_index], jnp.float32(0.0))
        total = total + weight[:, None] * picked
    return total.astype(jnp.bfloat16)
```

```python
import functools

import jax
import jax.numpy as jnp
import numpy as np
from jax import lax
from jax.experimental import pallas as pl
from jax.experimental.pallas import tpu as pltpu
from jax.sharding import PartitionSpec as P

MESH = pl.DeviceIdType.MESH
RING = 4
BLOCKS = 2 * RING
NT = 256
ORDERS = (("y", "x", "z"), ("x", "z", "y"), ("z", "y", "x"))


def chunk_widths(width):
    tiles = width // 128
    widths = [128 * ((tiles + 2 - r) // 3) for r in range(3)]
    return widths, [0, widths[0], widths[0] + widths[1]]


def swap_matrix(slots):
    unit = slots * BLOCKS
    q = np.arange(RING * unit)
    a, slot, c, b = q // unit, q % unit // BLOCKS, q % BLOCKS // RING, q % RING
    target = b * unit + slot * BLOCKS + c * RING + a
    return (np.arange(RING * unit)[:, None] == target[None, :]).astype(np.float32)


def column_tiles(width, body):
    full = width // NT

    @pl.loop(0, full)
    def _(n):
        body(pl.ds(pl.multiple_of(n * NT, NT), NT), NT)

    if width % NT:
        body(pl.ds(full * NT, width % NT), width % NT)


def kernel(slots, widths, starts, tok, meta, swap, wg, wu, wd, out,
           b2r0, b2r1, b2r2, b4r0, b4r1, b4r2, b5r0, b5r1, b5r2,
           g0, g1, g2, bs0, bs1, bs2, b30, b31, b32, sr0, sr1, sr2, rr0, rr1, rr2,
           km, kk, pp, sel, wc, comb, hid, hb, hc, wgv, wuv, wdv,
           wsem, own_sem, s1, r1, sm1, rm1, sf, rf, smf, rmf, s2, r2, s3, r3, l3,
           s4, r4, s5, r5, l5, ld5, s6, r6, s7, r7):
    b2r, b4r, b5r = (b2r0, b2r1, b2r2), (b4r0, b4r1, b4r2), (b5r0, b5r1, b5r2)
    g, bs, b3 = (g0, g1, g2), (bs0, bs1, bs2), (b30, b31, b32)
    sr, rr = (sr0, sr1, sr2), (rr0, rr1, rr2)
    unit = slots * BLOCKS
    rows = RING * unit
    toks = tok.shape[0]
    hidden = wdv.shape[0]
    grp, slc = lax.axis_index("grp"), lax.axis_index("slc")
    me = {"y": grp // 2, "c": lax.rem(grp, 2), "x": slc // RING, "z": lax.rem(slc, RING)}
    core = me["c"]
    mate = 1 - core

    def device(coords):
        return (coords["y"] * 2 + coords["c"], coords["x"] * RING + coords["z"])

    def at(**changes):
        return device({**me, **changes})

    def ahead(d, k):
        return lax.rem(me[d] + k, RING)

    def behind(d, k):
        return lax.rem(me[d] + RING - k, RING)

    def send(src, dst, ssem, rsem, where):
        return pltpu.make_async_remote_copy(
            src_ref=src, dst_ref=dst, send_sem=ssem, recv_sem=rsem, device_id=where, device_id_type=MESH
        )

    def local(src, dst, sem):
        return pltpu.make_async_copy(src, dst, sem)

    mate_id = at(c=mate)
    d1 = [o[0] for o in ORDERS]
    d2 = [o[1] for o in ORDERS]
    d3 = [o[2] for o in ORDERS]

    def w_in(n):
        cols = pl.ds(n * NT, NT)
        return (local(wg.at[:, cols], wgv.at[n % 2], wsem.at[2 * n]),
                local(wu.at[:, cols], wuv.at[n % 2], wsem.at[2 * n + 1]))

    h_tiles = hidden // NT
    for n in range(min(2, h_tiles)):
        for c in w_in(n):
            c.start()
    wd_in = local(wd, wdv, wsem.at[2 * h_tiles])
    wd_in.start()

    def tok_cols(r):
        return tok.at[:, pl.ds(starts[r], widths[r])]

    own_in = [local(tok_cols(r), g[r].at[core, me[d1[r]]], own_sem.at[r]) for r in range(3)]
    for c in own_in:
        c.start()

    barrier = pltpu.get_barrier_semaphore()
    greet = [mate_id] + [at(**{d: ahead(d, k)}) for d in ("x", "y", "z") for k in (1, 2, 3)]
    for where in greet:
        pl.semaphore_signal(barrier, inc=1, device_id=where, device_id_type=MESH)
    pl.semaphore_wait(barrier, len(greet))

    first, pending = [], []
    for r in range(3):
        mine = me[d1[r]]
        for i in range(3):
            where = at(**{d1[r]: ahead(d1[r], i + 1)})
            c = send(meta, km.at[r, core, mine], sm1.at[r, i], rm1.at[r, i], where)
            c.start()
            t = send(tok_cols(r), g[r].at[core, mine], s1.at[r, i], r1.at[r, i], where)
            t.start()
            first.append((r, i, c, t))
        c = send(meta, km.at[r, core, mine], smf.at[r, 0], rmf.at[r, 0], mate_id)
        c.start()
        t = send(tok_cols(r), g[r].at[core, mine], sf.at[r, 0], rf.at[r, 0], mate_id)
        t.start()
        pending += [c, t]
        km[r, core, mine] = meta[...]
    for i in range(3):
        for r in range(3):
            source = behind(d1[r], i + 1)
            _, _, c, t = first[3 * r + i]
            c.wait_recv()
            c2 = send(km.at[r, core, source], km.at[r, core, source], smf.at[r, i + 1], rmf.at[r, i + 1], mate_id)
            c2.start()
            t.wait_recv()
            t2 = send(g[r].at[core, source], g[r].at[core, source], sf.at[r, i + 1], rf.at[r, i + 1], mate_id)
            t2.start()
            pending += [c2, t2]
    for c in own_in:
        c.wait()
    for c in pending:
        c.wait_recv()
    for r in range(3):
        for k in range(8):
            kk[r, k] = jnp.concatenate([km[r, b // RING, b % RING, k : k + 1] for b in range(BLOCKS)], axis=0)
            pp[r, k] = jnp.concatenate([km[r, b // RING, b % RING, 8 + k : 9 + k] for b in range(BLOCKS)], axis=0)

    def route_key(r, p2, p3):
        place = {**me, d2[r]: p2, d3[r]: p3}
        expert = (place["y"] * 2 + core) * 16 + place["x"] * RING + place["z"]
        return expert * slots

    sub = lax.broadcasted_iota(jnp.int32, (BLOCKS, BLOCKS * toks), 0)
    lane = lax.broadcasted_iota(jnp.int32, (BLOCKS, BLOCKS * toks), 1)
    diagonal = (sub * toks <= lane) & (lane < sub * toks + toks)

    second = {}

    def dispatch(r, p2):
        @pl.loop(0, RING)
        def _(p3):
            base = route_key(r, p2, p3)
            keys = [kk[r, k] for k in range(8)]
            parts = []
            for slot in range(slots):
                key = (base + slot).astype(jnp.float32)
                hit = jnp.zeros((BLOCKS, toks), jnp.float32)
                for k in range(8):
                    hit = jnp.where(keys[k] == key, 1.0, hit)
                parts.append(jnp.where(diagonal, jnp.concatenate([hit] * BLOCKS, axis=1), 0.0))
            sel[pl.ds(pl.multiple_of(p3 * unit, unit), unit), :] = jnp.concatenate(parts, axis=0).astype(jnp.bfloat16)

        def tile(cols, size):
            data = g[r][:, :, :, cols].reshape(BLOCKS * toks, size)
            o = jnp.dot(sel[...], data, preferred_element_type=jnp.float32)
            bs[r][p2, :, :, cols] = o.astype(jnp.bfloat16).reshape(RING, unit, size)

        column_tiles(widths[r], tile)

    def second_send(r, i):
        p2 = ahead(d2[r], i + 1)
        return send(bs[r].at[p2], b2r[r].at[me[d2[r]]], s2.at[r, i], r2.at[r, i], at(**{d2[r]: p2}))

    @pl.loop(0, RING)
    def _(i):
        for r in range(3):
            dispatch(r, ahead(d2[r], i + 1))

            @pl.when(i < 3)
            def _():
                second_send(r, i).start()

    def third_source(r, i, p3):
        if i == 0:
            return bs[r].at[me[d2[r]], p3]
        return b2r[r].at[behind(d2[r], i), p3]

    def third_send(r, i, j):
        p3 = ahead(d3[r], j + 1)
        return send(third_source(r, i, p3), b3[r].at[me[d3[r]], behind(d2[r], i)],
                    s3.at[r, i, j], r3.at[r, i, j], at(**{d3[r]: p3}))

    def third_local(r, i):
        return local(third_source(r, i, me[d3[r]]), b3[r].at[me[d3[r]], behind(d2[r], i)], l3.at[r, i])

    for i in range(RING):
        for r in range(3):
            if i > 0:
                second_send(r, i - 1).wait_recv()
            for j in range(3):
                third_send(r, i, j).start()
            third_local(r, i).start()
    for i in range(RING):
        for r in range(3):
            third_local(r, i).wait()
            for j in range(3):
                third_send(r, i, j).wait_recv()

    def swap_rows(ref, index, width):
        def tile(cols, size):
            x = ref[(*index, slice(None), cols)].reshape(rows, size)
            y = jnp.dot(swap[...], x, preferred_element_type=jnp.float32)
            ref[(*index, slice(None), cols)] = y.astype(jnp.bfloat16).reshape(RING, unit, size)

        column_tiles(width, tile)

    @pl.loop(0, RING)
    def _(p):
        swap_rows(b3[1], (slice(None), p), widths[1])
        swap_rows(b3[2], (p, slice(None)), widths[2])

    for n in range(h_tiles):
        for c in w_in(n):
            c.wait()

        @pl.loop(0, RING)
        def _(p):
            gate = up = None
            for r in range(3):
                index = (p,) if r == 0 else (slice(None), p)
                x = b3[r][index].reshape(rows, widths[r])
                span = pl.ds(starts[r], widths[r])
                gr = jnp.dot(x, wgv[n % 2, span, :], preferred_element_type=jnp.float32)
                ur = jnp.dot(x, wuv[n % 2, span, :], preferred_element_type=jnp.float32)
                gate = gr if gate is None else gate + gr
                up = ur if up is None else up + ur
            h = gate / (1.0 + jnp.exp(-gate)) * up
            hid[p, :, :, n * NT : (n + 1) * NT] = h.astype(jnp.bfloat16).reshape(RING, unit, NT)

        if n + 2 < h_tiles:
            for c in w_in(n + 2):
                c.start()

    @pl.loop(0, RING)
    def _(p):
        x = hid[p].reshape(rows, hidden)
        y = jnp.dot(swap[...], x, preferred_element_type=jnp.float32)
        hb[:, p] = y.astype(jnp.bfloat16).reshape(RING, unit, hidden)
        x = hid[:, p].reshape(rows, hidden)
        y = jnp.dot(swap[...], x, preferred_element_type=jnp.float32)
        hc[p] = y.astype(jnp.bfloat16).reshape(RING, unit, hidden)

    wd_in.wait()
    for r in range(3):
        for i in range(3):
            second_send(r, i).wait_send()
            third_send(r, 0, i).wait_send()

    def fourth_send(r, i):
        p3 = ahead(d3[r], i + 1)
        return send(bs[r].at[p3], b4r[r].at[me[d3[r]]], s4.at[r, i], r4.at[r, i], at(**{d3[r]: p3}))

    @pl.loop(0, RING)
    def _(i):
        for r, h in enumerate((hid, hb, hc)):
            p3 = ahead(d3[r], i + 1)

            def tile(cols, size):
                x = h[p3].reshape(rows, hidden)
                w = wdv[:, pl.ds(pl.multiple_of(starts[r] + cols.start, 128), size)]
                o = jnp.dot(x, w, preferred_element_type=jnp.float32)
                bs[r][p3, :, :, cols] = o.astype(jnp.bfloat16).reshape(RING, unit, size)

            column_tiles(widths[r], tile)

            @pl.when(i < 3)
            def _():
                fourth_send(r, i).start()

    def fifth_source(r, i, p2):
        if i == 0:
            return bs[r].at[me[d3[r]], p2]
        return b4r[r].at[behind(d3[r], i), p2]

    def fifth_send(r, i, j):
        p2 = ahead(d2[r], j + 1)
        return send(fifth_source(r, i, p2), b5r[r].at[me[d2[r]], behind(d3[r], i)],
                    s5.at[r, i, j], r5.at[r, i, j], at(**{d2[r]: p2}))

    def fifth_local(r, i):
        return local(fifth_source(r, i, me[d2[r]]), b3[r].at[me[d2[r]], behind(d3[r], i)], l5.at[r, i])

    def fifth_load(r, i, j):
        e2, e3 = behind(d2[r], j + 1), behind(d3[r], i)
        return local(b5r[r].at[e2, e3], b3[r].at[e2, e3], ld5.at[r, i, j])

    for i in range(RING):
        for r in range(3):
            if i > 0:
                fourth_send(r, i - 1).wait_recv()
            for j in range(3):
                fifth_send(r, i, j).start()
            fifth_local(r, i).start()

    lanes = lax.broadcasted_iota(jnp.int32, (toks, RING * rows), 1)

    def sixth_send(r):
        return send(g[r].at[mate], sr[r], s6.at[r], r6.at[r], mate_id)

    for r in range(3):
        @pl.loop(0, RING * RING)
        def _(q):
            base = route_key(r, q // RING, lax.rem(q, RING))
            keys = [kk[r, k] for k in range(8)]
            probs = [pp[r, k] for k in range(8)]
            parts = []
            for slot in range(slots):
                key = (base + slot).astype(jnp.float32)
                weight = jnp.zeros((BLOCKS, toks), jnp.float32)
                for k in range(8):
                    weight = jnp.where(keys[k] == key, probs[k], weight)
                parts.append(weight)
            wc[pl.ds(pl.multiple_of(q * unit, unit), unit), :] = jnp.concatenate(parts, axis=0)

        turned = wc[...].T
        for b in range(BLOCKS):
            comb[b * toks : (b + 1) * toks, :] = jnp.where(lanes % BLOCKS == b, turned, 0.0).astype(jnp.bfloat16)

        for i in range(RING):
            for j in range(3):
                fifth_send(r, i, j).wait_recv()
                fifth_load(r, i, j).start()
        for c in pending[2 * r :: 6] + pending[2 * r + 1 :: 6]:
            c.wait_send()
        for i in range(RING):
            fifth_local(r, i).wait()
            for j in range(3):
                fifth_load(r, i, j).wait()

        def half(side):
            def tile(cols, size):
                x = b3[r][:, :, :, cols].reshape(RING * rows, size)
                w = comb[pl.ds(pl.multiple_of(side * RING * toks, RING * toks), RING * toks), :]
                o = jnp.dot(w, x, preferred_element_type=jnp.float32)
                g[r][side, :, :, cols] = o.astype(jnp.bfloat16).reshape(RING, toks, size)

            column_tiles(widths[r], tile)

        half(mate)
        sixth_send(r).start()
        half(core)

    def seventh_send(r, i):
        p1 = ahead(d1[r], i + 1)
        return send(g[r].at[core, p1], rr[r].at[i], s7.at[r, i], r7.at[r, i], at(**{d1[r]: p1}))

    for r in range(3):
        sixth_send(r).wait_recv()

        @pl.loop(0, RING)
        def _(i):
            p1 = ahead(d1[r], i + 1)
            total = g[r][core, p1].astype(jnp.float32) + sr[r][p1].astype(jnp.float32)
            g[r][core, p1] = total.astype(jnp.bfloat16)

            @pl.when(i < 3)
            def _():
                seventh_send(r, i).start()

    for r in range(3):
        total = g[r][core, me[d1[r]]].astype(jnp.float32)
        for i in range(3):
            seventh_send(r, i).wait_recv()
            total = total + rr[r][i].astype(jnp.float32)
        out[:, starts[r] : starts[r] + widths[r]] = total.astype(jnp.bfloat16)

    for _, _, c, t in first:
        c.wait_send()
        t.wait_send()
    for r in range(3):
        sixth_send(r).wait_send()
        for i in range(RING):
            for j in range(3):
                if i > 0:
                    third_send(r, i, j).wait_send()
                fifth_send(r, i, j).wait_send()
        for i in range(3):
            fourth_send(r, i).wait_send()
            seventh_send(r, i).wait_send()


def shards(tokens, expert_ids, slot_positions, gate_probs, w_gate, w_up, w_down):
    toks, width = tokens.shape
    experts = lax.axis_size(("grp", "slc"))
    slots = max(2, toks * expert_ids.shape[1] * 5 // (4 * experts))
    hidden = w_gate.shape[2]
    widths, starts = chunk_widths(width)
    unit = slots * BLOCKS
    keys = jnp.where(slot_positions < slots, expert_ids * slots + slot_positions, -1)
    meta = jnp.concatenate([keys.astype(jnp.float32).T, gate_probs.T], 0)
    swap = jnp.asarray(swap_matrix(slots), jnp.bfloat16)
    bf, f32 = jnp.bfloat16, jnp.float32
    hbm = [jax.ShapeDtypeStruct((RING, RING, unit, w), bf) for _ in range(3) for w in widths]
    dma = pltpu.SemaphoreType.DMA
    vmem = pltpu.VMEM
    scratch = (
        [vmem((2, RING, toks, w), bf) for w in widths]
        + [vmem((RING, RING, unit, w), bf) for w in widths]
        + [vmem((RING, RING, unit, w), bf) for w in widths]
        + [vmem((RING, toks, w), bf) for w in widths]
        + [vmem((3, toks, w), bf) for w in widths]
        + [
            vmem((3, 2, RING, 16, toks), f32),
            vmem((3, 8, BLOCKS, toks), f32),
            vmem((3, 8, BLOCKS, toks), f32),
            vmem((RING * unit, BLOCKS * toks), bf),
            vmem((RING * RING * unit, toks), f32),
            vmem((BLOCKS * toks, RING * RING * unit), bf),
            vmem((RING, RING, unit, hidden), bf),
            vmem((RING, RING, unit, hidden), bf),
            vmem((RING, RING, unit, hidden), bf),
            vmem((2, width, NT), bf),
            vmem((2, width, NT), bf),
            vmem((hidden, width), bf),
        ]
        + [dma((2 * (hidden // NT) + 1,)), dma((3,))]
        + [dma((3, 3))] * 4
        + [dma((3, 4))] * 4
        + [dma((3, 3))] * 2
        + [dma((3, 4, 3))] * 2
        + [dma((3, 4))]
        + [dma((3, 3))] * 2
        + [dma((3, 4, 3))] * 2
        + [dma((3, 4)), dma((3, 4, 3))]
        + [dma((3,))] * 2
        + [dma((3, 3))] * 2
    )
    any_spec = pl.BlockSpec(memory_space=pl.ANY)
    vmem_spec = pl.BlockSpec(memory_space=pltpu.VMEM)
    results = pl.pallas_call(
        functools.partial(kernel, slots, widths, starts),
        out_shape=[jax.ShapeDtypeStruct((toks, width), bf)] + hbm,
        in_specs=[any_spec, vmem_spec, vmem_spec, any_spec, any_spec, any_spec],
        out_specs=[vmem_spec] + [any_spec] * 9,
        scratch_shapes=scratch,
        compiler_params=pltpu.CompilerParams(
            collective_id=0, has_side_effects=True, vmem_limit_bytes=65000 * 1024
        ),
    )(tokens, meta, swap, w_gate.reshape(width, hidden), w_up.reshape(width, hidden), w_down.reshape(hidden, width))
    return results[0]


def solution(mesh):
    row = P(("grp", "slc"), None)
    cube = P(("grp", "slc"), None, None)
    return jax.shard_map(
        shards, mesh=mesh, in_specs=(row, row, row, row, cube, cube, cube), out_specs=row, check_vma=False
    )
```

```python
import functools

import jax
import jax.numpy as jnp
import numpy as np
from jax import lax
from jax.experimental import pallas as pl
from jax.experimental.pallas import tpu as pltpu
from jax.sharding import PartitionSpec as P

MESH = pl.DeviceIdType.MESH
RING = 4
BLOCKS = 2 * RING
NT = 256
ORDERS = (("y", "x", "z"), ("x", "z", "y"), ("z", "y", "x"))


def chunk_widths(width):
    tiles = width // 128
    widths = [128 * ((tiles + 2 - r) // 3) for r in range(3)]
    return widths, [0, widths[0], widths[0] + widths[1]]


def swap_matrix(slots):
    unit = slots * BLOCKS
    q = np.arange(RING * unit)
    a, slot, c, b = q // unit, q % unit // BLOCKS, q % BLOCKS // RING, q % RING
    target = b * unit + slot * BLOCKS + c * RING + a
    return (np.arange(RING * unit)[:, None] == target[None, :]).astype(np.float32)


def column_tiles(width):
    return [(n, min(NT, width - n)) for n in range(0, width, NT)]


def kernel(groups, widths, starts, tok, meta, swap0, swap1, wg, wu, wd, out, *refs):
    refs = list(refs)

    def take(count):
        taken, refs[:count] = refs[:count], []
        return taken

    b2r, b4r, b5r = ([take(3), take(3)] for _ in range(3))
    g = take(3)
    bs, b3 = ([take(3), take(3)] for _ in range(2))
    sr, rr = take(3), take(3)
    hid, hb, hc = (take(2) for _ in range(3))
    km, kk, pp, sel, wc, wgv, wuv, wdv = take(8)
    wsem, own_sem, s1, r1, sm1, rm1, sf, rf, smf, rmf = take(10)
    s2, r2, s3, r3, l3, s4, r4, s5, r5, l5, ld5, s6, r6, s7, r7 = take(15)
    swap = (swap0, swap1)
    units = [count * BLOCKS for _, count in groups]
    slots = sum(count for _, count in groups)
    toks = tok.shape[0]
    hidden = wdv.shape[0]
    grp, slc = lax.axis_index("grp"), lax.axis_index("slc")
    me = {"y": grp // 2, "c": lax.rem(grp, 2), "x": slc // RING, "z": lax.rem(slc, RING)}
    core = me["c"]
    mate = 1 - core

    def at(**changes):
        coords = {**me, **changes}
        return (coords["y"] * 2 + coords["c"], coords["x"] * RING + coords["z"])

    def ahead(d, k):
        return lax.rem(me[d] + k, RING)

    def behind(d, k):
        return lax.rem(me[d] + RING - k, RING)

    def send(src, dst, ssem, rsem, where):
        return pltpu.make_async_remote_copy(
            src_ref=src, dst_ref=dst, send_sem=ssem, recv_sem=rsem, device_id=where, device_id_type=MESH
        )

    def local(src, dst, sem):
        return pltpu.make_async_copy(src, dst, sem)

    mate_id = at(c=mate)
    d1 = [o[0] for o in ORDERS]
    d2 = [o[1] for o in ORDERS]
    d3 = [o[2] for o in ORDERS]
    h_tiles = hidden // NT
    uses = list(range(h_tiles)) + [(n + 1) % h_tiles for n in range(h_tiles)]
    places, loads = [], []
    held = {}
    for step, n in enumerate(uses):
        if n not in held:
            if len(held) < 2:
                place, after = len(held), -1
            else:
                oldest = uses[step - 2]
                place, after = held.pop(oldest), step - 2
            held[n] = place
            loads.append((step, n, place, after))
        places.append(held[n])

    def w_in(index):
        _, n, place, _ = loads[index]
        cols = pl.ds(n * NT, NT)
        return (local(wg.at[:, cols], wgv.at[place], wsem.at[2 * index]),
                local(wu.at[:, cols], wuv.at[place], wsem.at[2 * index + 1]))

    def loads_after(step):
        for index, (_, _, _, after) in enumerate(loads):
            if after == step:
                for c in w_in(index):
                    c.start()

    loads_after(-1)
    wd_in = local(wd, wdv, wsem.at[2 * len(loads)])
    wd_in.start()

    def tok_cols(r):
        return tok.at[:, pl.ds(starts[r], widths[r])]

    own_in = [local(tok_cols(r), g[r].at[core, me[d1[r]]], own_sem.at[r]) for r in range(3)]
    for c in own_in:
        c.start()

    barrier = pltpu.get_barrier_semaphore()
    greet = [mate_id] + [at(**{d: ahead(d, k)}) for d in ("x", "y", "z") for k in (1, 2, 3)]
    for where in greet:
        pl.semaphore_signal(barrier, inc=1, device_id=where, device_id_type=MESH)
    pl.semaphore_wait(barrier, len(greet))

    first, pending = [], []
    for r in range(3):
        mine = me[d1[r]]
        for i in range(3):
            where = at(**{d1[r]: ahead(d1[r], i + 1)})
            c = send(meta, km.at[r, core, mine], sm1.at[r, i], rm1.at[r, i], where)
            c.start()
            t = send(tok_cols(r), g[r].at[core, mine], s1.at[r, i], r1.at[r, i], where)
            t.start()
            first.append((c, t))
        c = send(meta, km.at[r, core, mine], smf.at[r, 0], rmf.at[r, 0], mate_id)
        c.start()
        t = send(tok_cols(r), g[r].at[core, mine], sf.at[r, 0], rf.at[r, 0], mate_id)
        t.start()
        pending += [c, t]
        km[r, core, mine] = meta[...]
    for i in range(3):
        for r in range(3):
            source = behind(d1[r], i + 1)
            c, t = first[3 * r + i]
            c.wait_recv()
            c2 = send(km.at[r, core, source], km.at[r, core, source], smf.at[r, i + 1], rmf.at[r, i + 1], mate_id)
            c2.start()
            t.wait_recv()
            t2 = send(g[r].at[core, source], g[r].at[core, source], sf.at[r, i + 1], rf.at[r, i + 1], mate_id)
            t2.start()
            pending += [c2, t2]
    for c in own_in:
        c.wait()
    for c in pending:
        c.wait_recv()
    for r in range(3):
        for k in range(8):
            kk[r, k] = jnp.concatenate([km[r, b // RING, b % RING, k : k + 1] for b in range(BLOCKS)], axis=0)
            pp[r, k] = jnp.concatenate([km[r, b // RING, b % RING, 8 + k : 9 + k] for b in range(BLOCKS)], axis=0)

    def route_key(r, p2, p3, slot):
        place = {**me, d2[r]: p2, d3[r]: p3}
        expert = (place["y"] * 2 + core) * 16 + place["x"] * RING + place["z"]
        return (expert * slots + slot).astype(jnp.float32)

    sub = lax.broadcasted_iota(jnp.int32, (BLOCKS, BLOCKS * toks), 0)
    lane = lax.broadcasted_iota(jnp.int32, (BLOCKS, BLOCKS * toks), 1)
    diagonal = (sub * toks <= lane) & (lane < sub * toks + toks)

    def second_send(a, r, i):
        p2 = ahead(d2[r], i + 1)
        return send(bs[a][r].at[p2], b2r[a][r].at[me[d2[r]]], s2.at[a, r, i], r2.at[a, r, i], at(**{d2[r]: p2}))

    def dispatch(a, r, pair):
        unit, (slot0, count) = units[a], groups[a]

        @pl.loop(0, 2 * RING)
        def _(q):
            p2 = jnp.where(q < RING, pair[0], pair[1])
            keys = [kk[r, k] for k in range(8)]
            parts = []
            for slot in range(count):
                key = route_key(r, p2, lax.rem(q, RING), slot0 + slot)
                hit = jnp.zeros((BLOCKS, toks), jnp.float32)
                for k in range(8):
                    hit = jnp.where(keys[k] == key, 1.0, hit)
                parts.append(jnp.where(diagonal, jnp.concatenate([hit] * BLOCKS, axis=1), 0.0))
            sel[pl.ds(pl.multiple_of(q * unit, unit), unit), :] = jnp.concatenate(parts, axis=0).astype(jnp.bfloat16)

        for n, size in column_tiles(widths[r]):
            data = g[r][:, :, :, n : n + size].reshape(BLOCKS * toks, size)
            o = jnp.dot(sel[: 2 * RING * unit], data, preferred_element_type=jnp.float32).astype(jnp.bfloat16)
            o = o.reshape(2, RING, unit, size)
            for e in range(2):
                bs[a][r][pair[e], :, :, n : n + size] = o[e]

    def dispatch_all(a, sending):
        @pl.loop(0, 2)
        def _(i):
            for r in range(3):
                dispatch(a, r, (ahead(d2[r], i + 1), ahead(d2[r], i + 3)))
                if sending:
                    @pl.when(i == 0)
                    def _():
                        second_send(a, r, 0).start()
                        second_send(a, r, 2).start()

                    @pl.when(i == 1)
                    def _():
                        second_send(a, r, 1).start()

    def third_source(a, r, i, p3):
        if i == 0:
            return bs[a][r].at[me[d2[r]], p3]
        return b2r[a][r].at[behind(d2[r], i), p3]

    def third_send(a, r, i, j):
        p3 = ahead(d3[r], j + 1)
        return send(third_source(a, r, i, p3), b3[a][r].at[me[d3[r]], behind(d2[r], i)],
                    s3.at[a, r, i, j], r3.at[a, r, i, j], at(**{d3[r]: p3}))

    def third_local(a, r, i):
        return local(third_source(a, r, i, me[d3[r]]), b3[a][r].at[me[d3[r]], behind(d2[r], i)], l3.at[a, r, i])

    def third_start(a, steps):
        for i in steps:
            for r in range(3):
                if i > 0:
                    second_send(a, r, i - 1).wait_recv()
                for j in range(3):
                    third_send(a, r, i, j).start()
                third_local(a, r, i).start()

    def third_finish(a):
        for i in range(RING):
            for r in range(3):
                third_local(a, r, i).wait()
                for j in range(3):
                    third_send(a, r, i, j).wait_recv()
        for r in range(3):
            for i in range(3):
                second_send(a, r, i).wait_send()
                third_send(a, r, 0, i).wait_send()

    def swap_rows(a):
        unit = units[a]

        @pl.loop(0, RING)
        def _(p):
            for n, size in column_tiles(widths[1]):
                x = b3[a][1][:, p, :, n : n + size].reshape(RING * unit, size)
                y = jnp.dot(swap[a][...], x, preferred_element_type=jnp.float32)
                bs[a][1][p, :, :, n : n + size] = y.astype(jnp.bfloat16).reshape(RING, unit, size)
            for n, size in column_tiles(widths[2]):
                x = b3[a][2][p, :, :, n : n + size].reshape(RING * unit, size)
                y = jnp.dot(swap[a][...], x, preferred_element_type=jnp.float32)
                bs[a][2][:, p, :, n : n + size] = y.astype(jnp.bfloat16).reshape(RING, unit, size)

    def up(a):
        unit = units[a]
        batch = 2
        for step in range(a * h_tiles, (a + 1) * h_tiles):
            n, place = uses[step], places[step]
            for index, (needed, _, _, _) in enumerate(loads):
                if needed == step:
                    for c in w_in(index):
                        c.wait()

            @pl.loop(0, RING // batch)
            def _(q):
                p = pl.ds(q * batch, batch)
                gate = lift = None
                for r, ref in enumerate((b3[a][0], bs[a][1], bs[a][2])):
                    x = ref[p].reshape(batch * RING * unit, widths[r])
                    span = pl.ds(starts[r], widths[r])
                    gr = jnp.dot(x, wgv[place, span, :], preferred_element_type=jnp.float32)
                    ur = jnp.dot(x, wuv[place, span, :], preferred_element_type=jnp.float32)
                    gate = gr if gate is None else gate + gr
                    lift = ur if lift is None else lift + ur
                h = gate / (1.0 + jnp.exp(-gate)) * lift
                hid[a][p, :, :, n * NT : (n + 1) * NT] = h.astype(jnp.bfloat16).reshape(batch, RING, unit, NT)

            loads_after(step)

    def swap_hidden(a):
        unit = units[a]

        @pl.loop(0, RING)
        def _(p):
            x = hid[a][p].reshape(RING * unit, hidden)
            y = jnp.dot(swap[a][...], x, preferred_element_type=jnp.float32)
            hb[a][:, p] = y.astype(jnp.bfloat16).reshape(RING, unit, hidden)
            x = hid[a][:, p].reshape(RING * unit, hidden)
            y = jnp.dot(swap[a][...], x, preferred_element_type=jnp.float32)
            hc[a][p] = y.astype(jnp.bfloat16).reshape(RING, unit, hidden)

    def fourth_send(a, r, i):
        p3 = ahead(d3[r], i + 1)
        return send(bs[a][r].at[p3], b4r[a][r].at[me[d3[r]]], s4.at[a, r, i], r4.at[a, r, i], at(**{d3[r]: p3}))

    def down(a):
        unit = units[a]

        @pl.loop(0, 2)
        def _(i):
            for r, h in enumerate((hid[a], hb[a], hc[a])):
                pair = (ahead(d3[r], i + 1), ahead(d3[r], i + 3))
                x = jnp.concatenate([h[p].reshape(RING * unit, hidden) for p in pair], axis=0)
                for n, size in column_tiles(widths[r]):
                    w = wdv[:, starts[r] + n : starts[r] + n + size]
                    o = jnp.dot(x, w, preferred_element_type=jnp.float32).astype(jnp.bfloat16)
                    o = o.reshape(2, RING, unit, size)
                    for e in range(2):
                        bs[a][r][pair[e], :, :, n : n + size] = o[e]

                @pl.when(i == 0)
                def _():
                    fourth_send(a, r, 0).start()
                    fourth_send(a, r, 2).start()

                @pl.when(i == 1)
                def _():
                    fourth_send(a, r, 1).start()

    def fifth_source(a, r, i, p2):
        if i == 0:
            return bs[a][r].at[me[d3[r]], p2]
        return b4r[a][r].at[behind(d3[r], i), p2]

    def fifth_send(a, r, i, j):
        p2 = ahead(d2[r], j + 1)
        return send(fifth_source(a, r, i, p2), b5r[a][r].at[me[d2[r]], behind(d3[r], i)],
                    s5.at[a, r, i, j], r5.at[a, r, i, j], at(**{d2[r]: p2}))

    def fifth_local(a, r, i):
        return local(fifth_source(a, r, i, me[d2[r]]), b3[a][r].at[me[d2[r]], behind(d3[r], i)], l5.at[a, r, i])

    def fifth_load(a, r, i, j):
        e2, e3 = behind(d2[r], j + 1), behind(d3[r], i)
        return local(b5r[a][r].at[e2, e3], b3[a][r].at[e2, e3], ld5.at[a, r, i, j])

    def fifth_start(a, steps):
        for i in steps:
            for r in range(3):
                if i > 0:
                    fourth_send(a, r, i - 1).wait_recv()
                for j in range(3):
                    fifth_send(a, r, i, j).start()
                fifth_local(a, r, i).start()

    def fifth_arrive(a, r):
        for i in range(RING):
            for j in range(3):
                fifth_send(a, r, i, j).wait_recv()
                fifth_load(a, r, i, j).start()

    def fifth_finish(a, r):
        for i in range(RING):
            fifth_local(a, r, i).wait()
            for j in range(3):
                fifth_load(a, r, i, j).wait()

    def weight_block(a, r, kb):
        if a == 0:
            return wgv.at[0, pl.ds(kb * BLOCKS * toks, BLOCKS * toks)]
        row = (2 * r + kb) * BLOCKS * toks
        return wuv.at[row // wuv.shape[1], pl.ds(row % wuv.shape[1], BLOCKS * toks)]

    def weigh(a, r):
        unit, (slot0, count) = units[a], groups[a]
        total = RING * RING * unit

        @pl.loop(0, RING * RING)
        def _(q):
            keys = [kk[r, k] for k in range(8)]
            probs = [pp[r, k] for k in range(8)]
            parts = []
            for slot in range(count):
                key = route_key(r, q // RING, lax.rem(q, RING), slot0 + slot)
                weight = jnp.zeros((BLOCKS, toks), jnp.float32)
                for k in range(8):
                    weight = jnp.where(keys[k] == key, probs[k], weight)
                parts.append(weight)
            wc[pl.ds(pl.multiple_of(q * unit, unit), unit), :] = jnp.concatenate(parts, axis=0)

        turned = wc[:total].T
        lanes = lax.broadcasted_iota(jnp.int32, (toks, NT), 1) % BLOCKS
        for kb in range(total // NT):
            part = turned[:, kb * NT : (kb + 1) * NT]
            target = weight_block(a, r, kb)
            for b in range(BLOCKS):
                target[b * toks : (b + 1) * toks, :] = jnp.where(lanes == b, part, 0.0).astype(jnp.bfloat16)

    def combine(a, r, side):
        rows = pl.ds(pl.multiple_of(side * RING * toks, RING * toks), RING * toks)
        blocks = RING * RING * units[a] // NT
        for n, size in column_tiles(widths[r]):
            x = b3[a][r][:, :, :, n : n + size].reshape(RING * RING * units[a], size)
            weights = jnp.concatenate([weight_block(a, r, kb)[rows, :] for kb in range(blocks)], axis=1)
            o = jnp.dot(weights, x, preferred_element_type=jnp.float32).reshape(RING, toks, size)
            if a:
                o = o + g[r][side, :, :, n : n + size].astype(jnp.float32)
            g[r][side, :, :, n : n + size] = o.astype(jnp.bfloat16)

    def sixth_send(r):
        return send(g[r].at[mate], sr[r], s6.at[r], r6.at[r], mate_id)

    def seventh_send(r, i):
        p1 = ahead(d1[r], i + 1)
        return send(g[r].at[core, p1], rr[r].at[i], s7.at[r, i], r7.at[r, i], at(**{d1[r]: p1}))

    dispatch_all(0, True)
    third_start(0, (0,))
    dispatch_all(1, False)
    third_start(0, (1, 2, 3))
    for r in range(3):
        for i in (0, 2, 1):
            second_send(1, r, i).start()
    third_start(1, (0,))
    third_finish(0)
    swap_rows(0)
    up(0)
    swap_hidden(0)
    wd_in.wait()
    third_start(1, (1, 2, 3))
    down(0)
    fifth_start(0, (0,))
    third_finish(1)
    swap_rows(1)
    up(1)
    swap_hidden(1)
    fifth_start(0, (1, 2, 3))
    down(1)
    fifth_start(1, (0,))
    for c in pending:
        c.wait_send()
    for r in range(3):
        weigh(1, r)
    for r in range(3):
        weigh(0, r)
        fifth_arrive(0, r)
        fifth_finish(0, r)
        combine(0, r, mate)
        combine(0, r, core)
    fifth_start(1, (1, 2, 3))
    for r in range(3):
        fifth_arrive(1, r)
        fifth_finish(1, r)
        combine(1, r, mate)
        sixth_send(r).start()
        combine(1, r, core)

    for r in range(3):
        sixth_send(r).wait_recv()

        @pl.loop(0, RING)
        def _(i):
            p1 = ahead(d1[r], i + 1)
            total = g[r][core, p1].astype(jnp.float32) + sr[r][p1].astype(jnp.float32)
            g[r][core, p1] = total.astype(jnp.bfloat16)

            @pl.when(i < 3)
            def _():
                seventh_send(r, i).start()

    for r in range(3):
        total = g[r][core, me[d1[r]]].astype(jnp.float32)
        for i in range(3):
            seventh_send(r, i).wait_recv()
            total = total + rr[r][i].astype(jnp.float32)
        out[:, starts[r] : starts[r] + widths[r]] = total.astype(jnp.bfloat16)

    for c, t in first:
        c.wait_send()
        t.wait_send()
    for r in range(3):
        sixth_send(r).wait_send()
        for i in range(3):
            seventh_send(r, i).wait_send()
        for a in range(2):
            for i in range(RING):
                for j in range(3):
                    if i > 0:
                        third_send(a, r, i, j).wait_send()
                    fifth_send(a, r, i, j).wait_send()
            for i in range(3):
                fourth_send(a, r, i).wait_send()


def shards(tokens, expert_ids, slot_positions, gate_probs, w_gate, w_up, w_down):
    toks, width = tokens.shape
    experts = lax.axis_size(("grp", "slc"))
    slots = max(2, toks * expert_ids.shape[1] * 5 // (4 * experts))
    lead = 2 * ((slots + 2) // 4)
    groups = ((0, lead), (lead, slots - lead))
    units = [count * BLOCKS for _, count in groups]
    hidden = w_gate.shape[2]
    widths, starts = chunk_widths(width)
    keys = jnp.where(slot_positions < slots, expert_ids * slots + slot_positions, -1)
    meta = jnp.concatenate([keys.astype(jnp.float32).T, gate_probs.T], 0)
    swaps = [jnp.asarray(swap_matrix(count), jnp.bfloat16) for _, count in groups]
    bf, f32 = jnp.bfloat16, jnp.float32
    hbm = [jax.ShapeDtypeStruct((RING, RING, u, w), bf) for _ in range(3) for u in units for w in widths]
    dma = pltpu.SemaphoreType.DMA
    vmem = pltpu.VMEM
    scratch = (
        [vmem((2, RING, toks, w), bf) for w in widths]
        + [vmem((RING, RING, u, w), bf) for _ in range(2) for u in units for w in widths]
        + [vmem((RING, toks, w), bf) for w in widths]
        + [vmem((3, toks, w), bf) for w in widths]
        + [vmem((RING, RING, u, hidden), bf) for _ in range(3) for u in units]
        + [
            vmem((3, 2, RING, 16, toks), f32),
            vmem((3, 8, BLOCKS, toks), f32),
            vmem((3, 8, BLOCKS, toks), f32),
            vmem((2 * RING * units[0], BLOCKS * toks), bf),
            vmem((RING * RING * units[0], toks), f32),
            vmem((2, width, NT), bf),
            vmem((2, width, NT), bf),
            vmem((hidden, width), bf),
        ]
        + [dma((16,)), dma((3,))]
        + [dma((3, 3))] * 4
        + [dma((3, 4))] * 4
        + [dma((2, 3, 3))] * 2
        + [dma((2, 3, 4, 3))] * 2
        + [dma((2, 3, 4))]
        + [dma((2, 3, 3))] * 2
        + [dma((2, 3, 4, 3))] * 2
        + [dma((2, 3, 4)), dma((2, 3, 4, 3))]
        + [dma((3,))] * 2
        + [dma((3, 3))] * 2
    )
    any_spec = pl.BlockSpec(memory_space=pl.ANY)
    vmem_spec = pl.BlockSpec(memory_space=pltpu.VMEM)
    results = pl.pallas_call(
        functools.partial(kernel, groups, widths, starts),
        out_shape=[jax.ShapeDtypeStruct((toks, width), bf)] + hbm,
        in_specs=[any_spec, vmem_spec, vmem_spec, vmem_spec, any_spec, any_spec, any_spec],
        out_specs=[vmem_spec] + [any_spec] * len(hbm),
        scratch_shapes=scratch,
        compiler_params=pltpu.CompilerParams(
            collective_id=0, has_side_effects=True, vmem_limit_bytes=65000 * 1024
        ),
    )(tokens, meta, *swaps, w_gate.reshape(width, hidden), w_up.reshape(width, hidden), w_down.reshape(hidden, width))
    return results[0]


def solution(mesh):
    row = P(("grp", "slc"), None)
    cube = P(("grp", "slc"), None, None)
    return jax.shard_map(
        shards, mesh=mesh, in_specs=(row, row, row, row, cube, cube, cube), out_specs=row, check_vma=False
    )
```

```python
import functools

import jax
import jax.numpy as jnp
import numpy as np
from jax import lax
from jax.experimental import pallas as pl
from jax.experimental.pallas import tpu as pltpu
from jax.sharding import PartitionSpec as P

MESH = pl.DeviceIdType.MESH
RING = 4
BLOCKS = 2 * RING
NT = 256
ORDERS = (("y", "x", "z"), ("x", "z", "y"), ("z", "y", "x"))


def chunk_widths(width):
    tiles = width // 128
    widths = [128 * ((tiles + 2 - r) // 3) for r in range(3)]
    return widths, [0, widths[0], widths[0] + widths[1]]


def swap_matrix(slots):
    unit = slots * BLOCKS
    q = np.arange(RING * unit)
    a, slot, c, b = q // unit, q % unit // BLOCKS, q % BLOCKS // RING, q % RING
    target = b * unit + slot * BLOCKS + c * RING + a
    return (np.arange(RING * unit)[:, None] == target[None, :]).astype(np.float32)


def column_tiles(width):
    return [(n, min(NT, width - n)) for n in range(0, width, NT)]


def kernel(groups, widths, starts, tok, ids, places_in, probs_in, swap0, swap1, wg, wu, wd, out, *refs):
    refs = list(refs)

    def take(count):
        taken, refs[:count] = refs[:count], []
        return taken

    b2r, b4r, b5r = ([take(3), take(3)] for _ in range(3))
    g = take(3)
    bs, b3 = ([take(3), take(3)] for _ in range(2))
    sr, rr = take(3), take(3)
    hid, hb, hc = (take(2) for _ in range(3))
    meta, km, kk, pp, sel, wc, wgv, wuv, wdv = take(9)
    wsem, own_sem, s1, r1, sb, rb, sm1, rm1, sf, rf, smf, rmf = take(12)
    s2, r2, s3, r3, l3, s4, r4, s5, r5, l5, ld5, s6, r6, s7, r7 = take(15)
    swap = (swap0, swap1)
    units = [count * BLOCKS for _, count in groups]
    slots = sum(count for _, count in groups)
    toks = tok.shape[0]
    hidden = wdv.shape[0]
    grp, slc = lax.axis_index("grp"), lax.axis_index("slc")
    me = {"y": grp // 2, "c": lax.rem(grp, 2), "x": slc // RING, "z": lax.rem(slc, RING)}
    core = me["c"]
    mate = 1 - core

    def at(**changes):
        coords = {**me, **changes}
        return (coords["y"] * 2 + coords["c"], coords["x"] * RING + coords["z"])

    def ahead(d, k):
        return lax.rem(me[d] + k, RING)

    def behind(d, k):
        return lax.rem(me[d] + RING - k, RING)

    def send(src, dst, ssem, rsem, where):
        return pltpu.make_async_remote_copy(
            src_ref=src, dst_ref=dst, send_sem=ssem, recv_sem=rsem, device_id=where, device_id_type=MESH
        )

    def local(src, dst, sem):
        return pltpu.make_async_copy(src, dst, sem)

    mate_id = at(c=mate)
    d1 = [o[0] for o in ORDERS]
    d2 = [o[1] for o in ORDERS]
    d3 = [o[2] for o in ORDERS]
    h_tiles = hidden // NT
    uses = list(range(h_tiles)) + [(n + 1) % h_tiles for n in range(h_tiles)]
    places, loads = [], []
    held = {}
    for step, n in enumerate(uses):
        if n not in held:
            if len(held) < 2:
                place, after = len(held), -1
            else:
                oldest = uses[step - 2]
                place, after = held.pop(oldest), step - 2
            held[n] = place
            loads.append((step, n, place, after))
        places.append(held[n])

    def w_in(index):
        _, n, place, _ = loads[index]
        cols = pl.ds(n * NT, NT)
        return (local(wg.at[:, cols], wgv.at[place], wsem.at[2 * index]),
                local(wu.at[:, cols], wuv.at[place], wsem.at[2 * index + 1]))

    def loads_after(step):
        for index, (_, _, _, after) in enumerate(loads):
            if after == step:
                for c in w_in(index):
                    c.start()

    chosen = jnp.where(places_in[...] < slots, ids[...] * slots + places_in[...], -1)
    meta[0:8] = chosen.astype(jnp.float32)
    meta[8:16] = probs_in[...]
    loads_after(-1)
    wd_in = local(wd, wdv, wsem.at[2 * len(loads)])
    wd_in.start()

    def tok_cols(r):
        return tok.at[:, pl.ds(starts[r], widths[r])]

    own_in = [local(tok_cols(r), g[r].at[core, me[d1[r]]], own_sem.at[r]) for r in range(3)]
    for c in own_in:
        c.start()

    barrier = pltpu.get_barrier_semaphore()
    greet = [mate_id] + [at(**{d: ahead(d, k)}) for d in ("x", "y", "z") for k in (1, 2, 3)]
    for where in greet:
        pl.semaphore_signal(barrier, inc=1, device_id=where, device_id_type=MESH)
    pl.semaphore_wait(barrier, len(greet))

    half = toks // 2
    lower, upper = pl.ds(0, half), pl.ds(half, half)
    ways = ((1, (lower, upper)), (3, (upper, lower)))
    first, pending, relays = [], [], []

    def to_mate(r, source, rows, index):
        ref = g[r].at[core, source, rows]
        c = send(ref, ref, sf.at[r, index], rf.at[r, index], mate_id)
        c.start()
        pending.append((r, c))

    routes = []
    for r in range(3):
        mine = me[d1[r]]
        for i in range(3):
            c = send(meta, km.at[r, core, mine], sm1.at[r, i], rm1.at[r, i], at(**{d1[r]: ahead(d1[r], i + 1)}))
            c.start()
            routes.append((r, i, c))
        c = send(meta, km.at[r, core, mine], smf.at[r, 0], rmf.at[r, 0], mate_id)
        c.start()
        pending.append((r, c))
    near = {}
    for h in range(2):
        for r in range(3):
            mine = me[d1[r]]
            for w, (way, halves) in enumerate(ways):
                src = tok.at[halves[h], pl.ds(starts[r], widths[r])]
                c = send(src, g[r].at[core, mine, halves[h]], s1.at[r, w, h], r1.at[r, w, h], at(**{d1[r]: ahead(d1[r], way)}))
                c.start()
                near[r, w, h] = c
    for r in range(3):
        mine = me[d1[r]]
        c = send(tok_cols(r), g[r].at[core, mine], sf.at[r, 0], rf.at[r, 0], mate_id)
        c.start()
        pending.append((r, c))
        km[r, core, mine] = meta[...]
    for h in range(2):
        for r in range(3):
            for w, (way, halves) in enumerate(ways):
                source = behind(d1[r], way)
                near[r, w, h].wait_recv()
                if h == 0:
                    ref = g[r].at[core, source, halves[0]]
                    c = send(ref, ref, sb.at[r, w], rb.at[r, w], at(**{d1[r]: ahead(d1[r], way)}))
                    c.start()
                    relays.append((r, w, c))
                to_mate(r, source, halves[h], 1 + 2 * w + h)
        if h == 0:
            for r, i, c in routes:
                source = behind(d1[r], i + 1)
                c.wait_recv()
                c = send(km.at[r, core, source], km.at[r, core, source], smf.at[r, i + 1], rmf.at[r, i + 1], mate_id)
                c.start()
                pending.append((r, c))
    for r, w, c in relays:
        c.wait_recv()
        to_mate(r, behind(d1[r], 2), ways[w][1][0], 5 + w)
    first = [c for _, _, c in routes] + list(near.values())
    for c in own_in:
        c.wait()
    for _, c in pending:
        c.wait_recv()
    for r in range(3):
        for k in range(8):
            kk[r, k] = jnp.concatenate([km[r, b // RING, b % RING, k : k + 1] for b in range(BLOCKS)], axis=0)
            pp[r, k] = jnp.concatenate([km[r, b // RING, b % RING, 8 + k : 9 + k] for b in range(BLOCKS)], axis=0)

    def route_key(r, p2, p3, slot):
        place = {**me, d2[r]: p2, d3[r]: p3}
        expert = (place["y"] * 2 + core) * 16 + place["x"] * RING + place["z"]
        return (expert * slots + slot).astype(jnp.float32)

    sub = lax.broadcasted_iota(jnp.int32, (BLOCKS, BLOCKS * toks), 0)
    lane = lax.broadcasted_iota(jnp.int32, (BLOCKS, BLOCKS * toks), 1)
    diagonal = (sub * toks <= lane) & (lane < sub * toks + toks)

    def second_send(a, r, i):
        p2 = ahead(d2[r], i + 1)
        return send(bs[a][r].at[p2], b2r[a][r].at[me[d2[r]]], s2.at[a, r, i], r2.at[a, r, i], at(**{d2[r]: p2}))

    def dispatch(a, r, pair):
        unit, (slot0, count) = units[a], groups[a]

        @pl.loop(0, 2 * RING)
        def _(q):
            p2 = jnp.where(q < RING, pair[0], pair[1])
            keys = [kk[r, k] for k in range(8)]
            parts = []
            for slot in range(count):
                key = route_key(r, p2, lax.rem(q, RING), slot0 + slot)
                hit = jnp.zeros((BLOCKS, toks), jnp.float32)
                for k in range(8):
                    hit = jnp.where(keys[k] == key, 1.0, hit)
                parts.append(jnp.where(diagonal, jnp.concatenate([hit] * BLOCKS, axis=1), 0.0))
            sel[pl.ds(pl.multiple_of(q * unit, unit), unit), :] = jnp.concatenate(parts, axis=0).astype(jnp.bfloat16)

        for n, size in column_tiles(widths[r]):
            data = g[r][:, :, :, n : n + size].reshape(BLOCKS * toks, size)
            o = jnp.dot(sel[: 2 * RING * unit], data, preferred_element_type=jnp.float32).astype(jnp.bfloat16)
            o = o.reshape(2, RING, unit, size)
            for e in range(2):
                bs[a][r][pair[e], :, :, n : n + size] = o[e]

    def dispatch_all(a, sending):
        @pl.loop(0, 2)
        def _(i):
            for r in range(3):
                dispatch(a, r, (ahead(d2[r], i + 1), ahead(d2[r], i + 3)))
                if sending:
                    @pl.when(i == 0)
                    def _():
                        second_send(a, r, 0).start()
                        second_send(a, r, 2).start()

                    @pl.when(i == 1)
                    def _():
                        second_send(a, r, 1).start()

    def third_source(a, r, i, p3):
        if i == 0:
            return bs[a][r].at[me[d2[r]], p3]
        return b2r[a][r].at[behind(d2[r], i), p3]

    def third_send(a, r, i, j):
        p3 = ahead(d3[r], j + 1)
        return send(third_source(a, r, i, p3), b3[a][r].at[me[d3[r]], behind(d2[r], i)],
                    s3.at[a, r, i, j], r3.at[a, r, i, j], at(**{d3[r]: p3}))

    def third_local(a, r, i):
        return local(third_source(a, r, i, me[d3[r]]), b3[a][r].at[me[d3[r]], behind(d2[r], i)], l3.at[a, r, i])

    def third_start(a, steps):
        for i in steps:
            for r in range(3):
                if i > 0:
                    second_send(a, r, i - 1).wait_recv()
                for j in range(3):
                    third_send(a, r, i, j).start()
                third_local(a, r, i).start()

    def third_finish(a):
        for i in range(RING):
            for r in range(3):
                third_local(a, r, i).wait()
                for j in range(3):
                    third_send(a, r, i, j).wait_recv()
        for r in range(3):
            for i in range(3):
                second_send(a, r, i).wait_send()
                third_send(a, r, 0, i).wait_send()

    def swap_rows(a):
        unit = units[a]

        @pl.loop(0, RING)
        def _(p):
            for n, size in column_tiles(widths[1]):
                x = b3[a][1][:, p, :, n : n + size].reshape(RING * unit, size)
                y = jnp.dot(swap[a][...], x, preferred_element_type=jnp.float32)
                bs[a][1][p, :, :, n : n + size] = y.astype(jnp.bfloat16).reshape(RING, unit, size)
            for n, size in column_tiles(widths[2]):
                x = b3[a][2][p, :, :, n : n + size].reshape(RING * unit, size)
                y = jnp.dot(swap[a][...], x, preferred_element_type=jnp.float32)
                bs[a][2][:, p, :, n : n + size] = y.astype(jnp.bfloat16).reshape(RING, unit, size)

    def up(a):
        unit = units[a]
        batch = 2
        for step in range(a * h_tiles, (a + 1) * h_tiles):
            n, place = uses[step], places[step]
            for index, (needed, _, _, _) in enumerate(loads):
                if needed == step:
                    for c in w_in(index):
                        c.wait()

            @pl.loop(0, RING // batch)
            def _(q):
                p = pl.ds(q * batch, batch)
                gate = lift = None
                for r, ref in enumerate((b3[a][0], bs[a][1], bs[a][2])):
                    x = ref[p].reshape(batch * RING * unit, widths[r])
                    span = pl.ds(starts[r], widths[r])
                    gr = jnp.dot(x, wgv[place, span, :], preferred_element_type=jnp.float32)
                    ur = jnp.dot(x, wuv[place, span, :], preferred_element_type=jnp.float32)
                    gate = gr if gate is None else gate + gr
                    lift = ur if lift is None else lift + ur
                h = gate / (1.0 + jnp.exp(-gate)) * lift
                hid[a][p, :, :, n * NT : (n + 1) * NT] = h.astype(jnp.bfloat16).reshape(batch, RING, unit, NT)

            loads_after(step)

    def swap_hidden(a):
        unit = units[a]

        @pl.loop(0, RING)
        def _(p):
            x = hid[a][p].reshape(RING * unit, hidden)
            y = jnp.dot(swap[a][...], x, preferred_element_type=jnp.float32)
            hb[a][:, p] = y.astype(jnp.bfloat16).reshape(RING, unit, hidden)
            x = hid[a][:, p].reshape(RING * unit, hidden)
            y = jnp.dot(swap[a][...], x, preferred_element_type=jnp.float32)
            hc[a][p] = y.astype(jnp.bfloat16).reshape(RING, unit, hidden)

    def part_tiles(r, part):
        tiles = column_tiles(widths[r])
        middle = (len(tiles) + 1) // 2
        return tiles[:middle] if part == 0 else tiles[middle:]

    def part_cols(r, part):
        tiles = part_tiles(r, part)
        return tiles[0][0], tiles[-1][0] + tiles[-1][1] - tiles[0][0]

    def back_tiles(a, r, part):
        return part_tiles(r, part) if a else column_tiles(widths[r])

    def back_cols(a, r, part):
        return pl.ds(*part_cols(r, part)) if a else pl.ds(0, widths[r])

    def fourth_send(a, part, r, i):
        p3 = ahead(d3[r], i + 1)
        cols = back_cols(a, r, part)
        return send(bs[a][r].at[p3, :, :, cols], b4r[a][r].at[me[d3[r]], :, :, cols],
                    s4.at[a + part, r, i], r4.at[a + part, r, i], at(**{d3[r]: p3}))

    def down(a, part):
        unit = units[a]

        @pl.loop(0, 2)
        def _(i):
            for r, h in enumerate((hid[a], hb[a], hc[a])):
                pair = (ahead(d3[r], i + 1), ahead(d3[r], i + 3))
                x = jnp.concatenate([h[p].reshape(RING * unit, hidden) for p in pair], axis=0)
                for n, size in back_tiles(a, r, part):
                    w = wdv[:, starts[r] + n : starts[r] + n + size]
                    o = jnp.dot(x, w, preferred_element_type=jnp.float32).astype(jnp.bfloat16)
                    o = o.reshape(2, RING, unit, size)
                    for e in range(2):
                        bs[a][r][pair[e], :, :, n : n + size] = o[e]

                @pl.when(i == 0)
                def _():
                    fourth_send(a, part, r, 0).start()
                    fourth_send(a, part, r, 2).start()

                @pl.when(i == 1)
                def _():
                    fourth_send(a, part, r, 1).start()

    def fifth_source(a, part, r, i, p2):
        cols = back_cols(a, r, part)
        if i == 0:
            return bs[a][r].at[me[d3[r]], p2, :, cols]
        return b4r[a][r].at[behind(d3[r], i), p2, :, cols]

    def fifth_send(a, part, r, i, j):
        p2 = ahead(d2[r], j + 1)
        return send(fifth_source(a, part, r, i, p2), b5r[a][r].at[me[d2[r]], behind(d3[r], i), :, back_cols(a, r, part)],
                    s5.at[a + part, r, i, j], r5.at[a + part, r, i, j], at(**{d2[r]: p2}))

    def fifth_local(a, part, r, i):
        mine = me[d2[r]]
        return local(fifth_source(a, part, r, i, mine), b3[a][r].at[mine, behind(d3[r], i), :, back_cols(a, r, part)],
                     l5.at[a + part, r, i])

    def fifth_load(a, part, r, i, j):
        e2, e3, cols = behind(d2[r], j + 1), behind(d3[r], i), back_cols(a, r, part)
        return local(b5r[a][r].at[e2, e3, :, cols], b3[a][r].at[e2, e3, :, cols], ld5.at[a + part, r, i, j])

    def fifth_start(a, part, steps):
        for i in steps:
            for r in range(3):
                if i > 0:
                    fourth_send(a, part, r, i - 1).wait_recv()
                for j in range(3):
                    fifth_send(a, part, r, i, j).start()
                fifth_local(a, part, r, i).start()

    def fifth_arrive(a, part, r):
        for i in range(RING):
            for j in range(3):
                fifth_send(a, part, r, i, j).wait_recv()
                fifth_load(a, part, r, i, j).start()

    def fifth_finish(a, part, r):
        for i in range(RING):
            fifth_local(a, part, r, i).wait()
            for j in range(3):
                fifth_load(a, part, r, i, j).wait()

    def weight_block(a, r, kb):
        if a == 0:
            return wgv.at[0, pl.ds(kb * BLOCKS * toks, BLOCKS * toks)]
        row = (2 * r + kb) * BLOCKS * toks
        return wuv.at[row // wuv.shape[1], pl.ds(row % wuv.shape[1], BLOCKS * toks)]

    def weigh(a, r):
        unit, (slot0, count) = units[a], groups[a]
        total = RING * RING * unit

        @pl.loop(0, RING * RING)
        def _(q):
            keys = [kk[r, k] for k in range(8)]
            probs = [pp[r, k] for k in range(8)]
            parts = []
            for slot in range(count):
                key = route_key(r, q // RING, lax.rem(q, RING), slot0 + slot)
                weight = jnp.zeros((BLOCKS, toks), jnp.float32)
                for k in range(8):
                    weight = jnp.where(keys[k] == key, probs[k], weight)
                parts.append(weight)
            wc[pl.ds(pl.multiple_of(q * unit, unit), unit), :] = jnp.concatenate(parts, axis=0)

        turned = wc[:total].T
        lanes = lax.broadcasted_iota(jnp.int32, (toks, NT), 1) % BLOCKS
        for kb in range(total // NT):
            part = turned[:, kb * NT : (kb + 1) * NT]
            target = weight_block(a, r, kb)
            for b in range(BLOCKS):
                target[b * toks : (b + 1) * toks, :] = jnp.where(lanes == b, part, 0.0).astype(jnp.bfloat16)

    def combine(a, r, side, tiles):
        rows = pl.ds(pl.multiple_of(side * RING * toks, RING * toks), RING * toks)
        blocks = RING * RING * units[a] // NT
        for n, size in tiles:
            x = b3[a][r][:, :, :, n : n + size].reshape(RING * RING * units[a], size)
            weights = jnp.concatenate([weight_block(a, r, kb)[rows, :] for kb in range(blocks)], axis=1)
            o = jnp.dot(weights, x, preferred_element_type=jnp.float32).reshape(RING, toks, size)
            if a:
                o = o + g[r][side, :, :, n : n + size].astype(jnp.float32)
            g[r][side, :, :, n : n + size] = o.astype(jnp.bfloat16)

    def sixth_send(r, part):
        cols = pl.ds(*part_cols(r, part))
        return send(g[r].at[mate, :, :, cols], sr[r].at[:, :, cols], s6.at[r, part], r6.at[r, part], mate_id)

    def seventh_send(r, part, i):
        p1 = ahead(d1[r], i + 1)
        n, size = part_cols(r, part)
        return send(g[r].at[core, p1, :, pl.ds(n, size)], rr[r].at[i, :, pl.ds(n, size)],
                    s7.at[r, part, i], r7.at[r, part, i], at(**{d1[r]: p1}))

    dispatch_all(0, True)
    third_start(0, (0,))
    dispatch_all(1, False)
    third_start(0, (1, 2, 3))
    for r in range(3):
        for i in (0, 2, 1):
            second_send(1, r, i).start()
    third_start(1, (0,))
    third_finish(0)
    swap_rows(0)
    up(0)
    swap_hidden(0)
    wd_in.wait()
    third_start(1, (1, 2, 3))
    down(0, 0)
    fifth_start(0, 0, (0,))
    third_finish(1)
    swap_rows(1)
    up(1)
    swap_hidden(1)
    fifth_start(0, 0, (1, 2, 3))
    for part in range(2):
        down(1, part)
        fifth_start(1, part, (0,))
    for c in [c for _, c in pending] + [c for _, _, c in relays]:
        c.wait_send()
    for r in range(3):
        weigh(1, r)
    for r in range(3):
        weigh(0, r)
        fifth_arrive(0, 0, r)
        fifth_finish(0, 0, r)
        combine(0, r, mate, column_tiles(widths[r]))
        combine(0, r, core, column_tiles(widths[r]))
    for part in range(2):
        fifth_start(1, part, (1, 2, 3))

    for part in range(2):
        for r in range(3):
            fifth_arrive(1, part, r)
        for r in range(3):
            fifth_finish(1, part, r)
            combine(1, r, mate, part_tiles(r, part))
            sixth_send(r, part).start()
        for r in range(3):
            combine(1, r, core, part_tiles(r, part))
        for r in range(3):
            sixth_send(r, part).wait_recv()
            n, size = part_cols(r, part)

            for i in range(3):
                p1 = ahead(d1[r], i + 1)
                total = g[r][core, p1, :, n : n + size].astype(jnp.float32) + sr[r][p1, :, n : n + size].astype(jnp.float32)
                g[r][core, p1, :, n : n + size] = total.astype(jnp.bfloat16)
                seventh_send(r, part, i).start()

    for part in range(2):
        for r in range(3):
            n, size = part_cols(r, part)
            mine = me[d1[r]]
            total = g[r][core, mine, :, n : n + size].astype(jnp.float32) + sr[r][mine, :, n : n + size].astype(jnp.float32)
            for i in range(3):
                seventh_send(r, part, i).wait_recv()
                total = total + rr[r][i, :, n : n + size].astype(jnp.float32)
            out[:, starts[r] + n : starts[r] + n + size] = total.astype(jnp.bfloat16)

    for r in range(3):
        for part in range(2):
            sixth_send(r, part).wait_send()
            for i in range(3):
                seventh_send(r, part, i).wait_send()
    for c in first:
        c.wait_send()
    for r in range(3):
        for a in range(2):
            for i in range(RING):
                for j in range(3):
                    if i > 0:
                        third_send(a, r, i, j).wait_send()
                    for part in range(1 + a):
                        fifth_send(a, part, r, i, j).wait_send()
            for i in range(3):
                for part in range(1 + a):
                    fourth_send(a, part, r, i).wait_send()


def shards(tokens, expert_ids, slot_positions, gate_probs, w_gate, w_up, w_down):
    toks, width = tokens.shape
    experts = lax.axis_size(("grp", "slc"))
    slots = max(2, toks * expert_ids.shape[1] * 5 // (4 * experts))
    lead = 2 * ((slots + 2) // 4)
    groups = ((0, lead), (lead, slots - lead))
    units = [count * BLOCKS for _, count in groups]
    hidden = w_gate.shape[2]
    widths, starts = chunk_widths(width)
    swaps = [jnp.asarray(swap_matrix(count), jnp.bfloat16) for _, count in groups]
    bf, f32 = jnp.bfloat16, jnp.float32
    hbm = [jax.ShapeDtypeStruct((RING, RING, u, w), bf) for _ in range(3) for u in units for w in widths]
    dma = pltpu.SemaphoreType.DMA
    vmem = pltpu.VMEM
    scratch = (
        [vmem((2, RING, toks, w), bf) for w in widths]
        + [vmem((RING, RING, u, w), bf) for _ in range(2) for u in units for w in widths]
        + [vmem((RING, toks, w), bf) for w in widths]
        + [vmem((3, toks, w), bf) for w in widths]
        + [vmem((RING, RING, u, hidden), bf) for _ in range(3) for u in units]
        + [
            vmem((16, toks), f32),
            vmem((3, 2, RING, 16, toks), f32),
            vmem((3, 8, BLOCKS, toks), f32),
            vmem((3, 8, BLOCKS, toks), f32),
            vmem((2 * RING * units[0], BLOCKS * toks), bf),
            vmem((RING * RING * units[0], toks), f32),
            vmem((2, width, NT), bf),
            vmem((2, width, NT), bf),
            vmem((hidden, width), bf),
        ]
        + [dma((16,)), dma((3,))]
        + [dma((3, 2, 2))] * 2
        + [dma((3, 2))] * 2
        + [dma((3, 3))] * 2
        + [dma((3, 7))] * 2
        + [dma((3, 4))] * 2
        + [dma((2, 3, 3))] * 2
        + [dma((2, 3, 4, 3))] * 2
        + [dma((2, 3, 4))]
        + [dma((3, 3, 3))] * 2
        + [dma((3, 3, 4, 3))] * 2
        + [dma((3, 3, 4)), dma((3, 3, 4, 3))]
        + [dma((3, 2))] * 2
        + [dma((3, 2, 3))] * 2
    )
    any_spec = pl.BlockSpec(memory_space=pl.ANY)
    vmem_spec = pl.BlockSpec(memory_space=pltpu.VMEM)
    results = pl.pallas_call(
        functools.partial(kernel, groups, widths, starts),
        out_shape=[jax.ShapeDtypeStruct((toks, width), bf)] + hbm,
        in_specs=[any_spec] + [vmem_spec] * 5 + [any_spec] * 3,
        out_specs=[vmem_spec] + [any_spec] * len(hbm),
        scratch_shapes=scratch,
        compiler_params=pltpu.CompilerParams(
            collective_id=0, has_side_effects=True, vmem_limit_bytes=65000 * 1024
        ),
    )(tokens, expert_ids.T, slot_positions.T, gate_probs.T, *swaps,
      w_gate.reshape(width, hidden), w_up.reshape(width, hidden), w_down.reshape(hidden, width))
    return results[0]


def solution(mesh):
    row = P(("grp", "slc"), None)
    cube = P(("grp", "slc"), None, None)
    return jax.shard_map(
        shards, mesh=mesh, in_specs=(row, row, row, row, cube, cube, cube), out_specs=row, check_vma=False
    )
```

```python
import functools

import jax
import jax.numpy as jnp
import numpy as np
from jax import lax
from jax.experimental import pallas as pl
from jax.experimental.pallas import tpu as pltpu
from jax.sharding import PartitionSpec as P

MESH = pl.DeviceIdType.MESH
RING = 4
BLOCKS = 2 * RING
NT = 256
ORDERS = (("y", "x", "z"), ("x", "z", "y"), ("z", "y", "x"))


def chunk_widths(width):
    tiles = width // 128
    widths = [128 * ((tiles + 2 - r) // 3) for r in range(3)]
    return widths, [0, widths[0], widths[0] + widths[1]]


def swap_matrix(slots):
    unit = slots * BLOCKS
    q = np.arange(RING * unit)
    a, slot, c, b = q // unit, q % unit // BLOCKS, q % BLOCKS // RING, q % RING
    target = b * unit + slot * BLOCKS + c * RING + a
    return (np.arange(RING * unit)[:, None] == target[None, :]).astype(np.float32)


def column_tiles(width):
    return [(n, min(NT, width - n)) for n in range(0, width, NT)]


def kernel(groups, widths, starts, tok, ids, places_in, probs_in, swap0, swap1, wg, wu, wd, out, *refs):
    refs = list(refs)

    def take(count):
        taken, refs[:count] = refs[:count], []
        return taken

    b2r, b4r, b5r = ([take(3), take(3)] for _ in range(3))
    g = take(3)
    bs, b3 = ([take(3), take(3)] for _ in range(2))
    sr, rr = take(3), take(3)
    hid, hb, hc = (take(2) for _ in range(3))
    meta, km, kk, pp, sel, wc, wgv, wuv, wdv = take(9)
    wsem, own_sem, s1, r1, sb, rb, sm1, rm1, sf, rf, smf, rmf = take(12)
    s2, r2, s3, r3, l3, s4, r4, s5, r5, l5, ld5, s6, r6, s7, r7 = take(15)
    swap = (swap0, swap1)
    units = [count * BLOCKS for _, count in groups]
    slots = sum(count for _, count in groups)
    toks = tok.shape[0]
    hidden = wdv.shape[0]
    grp, slc = lax.axis_index("grp"), lax.axis_index("slc")
    me = {"y": grp // 2, "c": lax.rem(grp, 2), "x": slc // RING, "z": lax.rem(slc, RING)}
    core = me["c"]
    mate = 1 - core

    def at(**changes):
        coords = {**me, **changes}
        return (coords["y"] * 2 + coords["c"], coords["x"] * RING + coords["z"])

    def ahead(d, k):
        return lax.rem(me[d] + k, RING)

    def behind(d, k):
        return lax.rem(me[d] + RING - k, RING)

    def send(src, dst, ssem, rsem, where):
        return pltpu.make_async_remote_copy(
            src_ref=src, dst_ref=dst, send_sem=ssem, recv_sem=rsem, device_id=where, device_id_type=MESH
        )

    def local(src, dst, sem):
        return pltpu.make_async_copy(src, dst, sem)

    mate_id = at(c=mate)
    d1 = [o[0] for o in ORDERS]
    d2 = [o[1] for o in ORDERS]
    d3 = [o[2] for o in ORDERS]
    h_tiles = hidden // NT
    uses = list(range(h_tiles)) + [(n + 1) % h_tiles for n in range(h_tiles)]
    places, loads = [], []
    held = {}
    for step, n in enumerate(uses):
        if n not in held:
            if len(held) < 2:
                place, after = len(held), -1
            else:
                oldest = uses[step - 2]
                place, after = held.pop(oldest), step - 2
            held[n] = place
            loads.append((step, n, place, after))
        places.append(held[n])

    def w_in(index):
        _, n, place, _ = loads[index]
        cols = pl.ds(n * NT, NT)
        return (local(wg.at[:, cols], wgv.at[place], wsem.at[2 * index]),
                local(wu.at[:, cols], wuv.at[place], wsem.at[2 * index + 1]))

    def loads_after(step):
        for index, (_, _, _, after) in enumerate(loads):
            if after == step:
                for c in w_in(index):
                    c.start()

    chosen = jnp.where(places_in[...] < slots, ids[...] * slots + places_in[...], -1)
    meta[0:8] = chosen.astype(jnp.float32)
    meta[8:16] = probs_in[...]
    loads_after(-1)
    wd_in = local(wd, wdv, wsem.at[2 * len(loads)])
    wd_in.start()

    def tok_cols(r):
        return tok.at[:, pl.ds(starts[r], widths[r])]

    own_in = [local(tok_cols(r), g[r].at[core, me[d1[r]]], own_sem.at[r]) for r in range(3)]
    for c in own_in:
        c.start()

    barrier = pltpu.get_barrier_semaphore()
    greet = [mate_id] + [at(**{d: ahead(d, k)}) for d in ("x", "y", "z") for k in (1, 2, 3)]
    for where in greet:
        pl.semaphore_signal(barrier, inc=1, device_id=where, device_id_type=MESH)
    pl.semaphore_wait(barrier, len(greet))

    def part_tiles(r, part):
        tiles = column_tiles(widths[r])
        middle = (len(tiles) + 1) // 2
        return tiles[:middle] if part == 0 else tiles[middle:]

    def part_cols(r, part):
        tiles = part_tiles(r, part)
        return tiles[0][0], tiles[-1][0] + tiles[-1][1] - tiles[0][0]

    ways = ((1, pl.ds(0, toks // 2)), (3, pl.ds(toks // 2, toks // 2)))

    def near_send(part, r, w):
        n, size = part_cols(r, part)
        return send(tok.at[:, pl.ds(starts[r] + n, size)], g[r].at[core, me[d1[r]], :, pl.ds(n, size)],
                    s1.at[part, r, w], r1.at[part, r, w], at(**{d1[r]: ahead(d1[r], ways[w][0])}))

    def relay_send(part, r, w):
        way, rows = ways[w]
        ref = g[r].at[core, behind(d1[r], way), rows, pl.ds(*part_cols(r, part))]
        return send(ref, ref, sb.at[part, r, w], rb.at[part, r, w], at(**{d1[r]: ahead(d1[r], way)}))

    def mate_send(part, r, k):
        n, size = part_cols(r, part)
        cols = pl.ds(n, size)
        if k == 0:
            src, dst = tok.at[:, pl.ds(starts[r] + n, size)], g[r].at[core, me[d1[r]], :, cols]
        elif k < 3:
            src = dst = g[r].at[core, behind(d1[r], ways[k - 1][0]), :, cols]
        else:
            src = dst = g[r].at[core, behind(d1[r], 2), ways[k - 3][1], cols]
        return send(src, dst, sf.at[part, r, k], rf.at[part, r, k], mate_id)

    def route_send(r, i):
        return send(meta, km.at[r, core, me[d1[r]]], sm1.at[r, i], rm1.at[r, i], at(**{d1[r]: ahead(d1[r], i + 1)}))

    def route_mate(r, i):
        src = km.at[r, core, behind(d1[r], i)] if i else meta
        return send(src, km.at[r, core, behind(d1[r], i)], smf.at[r, i], rmf.at[r, i], mate_id)

    def near_step(part):
        for r in range(3):
            for w in range(2):
                near_send(part, r, w).wait_recv()
                relay_send(part, r, w).start()
                if part == 0:
                    near_send(1, r, w).start()
        for r in range(3):
            for w in range(2):
                mate_send(part, r, 1 + w).start()

    def relay_step(part):
        for r in range(3):
            for w in range(2):
                relay_send(part, r, w).wait_recv()
                mate_send(part, r, 3 + w).start()
        for r in range(3):
            for k in range(5):
                mate_send(part, r, k).wait_recv()

    for r in range(3):
        for i in range(3):
            route_send(r, i).start()
        route_mate(r, 0).start()
    for r in range(3):
        for w in range(2):
            near_send(0, r, w).start()
    for part in range(2):
        for r in range(3):
            mate_send(part, r, 0).start()
    for r in range(3):
        km[r, core, me[d1[r]]] = meta[...]
    near_step(0)
    for r in range(3):
        for i in range(3):
            route_send(r, i).wait_recv()
            route_mate(r, i + 1).start()
    for r in range(3):
        for i in range(4):
            route_mate(r, i).wait_recv()
    relay_step(0)
    for c in own_in:
        c.wait()
    for r in range(3):
        for k in range(8):
            kk[r, k] = jnp.concatenate([km[r, b // RING, b % RING, k : k + 1] for b in range(BLOCKS)], axis=0)
            pp[r, k] = jnp.concatenate([km[r, b // RING, b % RING, 8 + k : 9 + k] for b in range(BLOCKS)], axis=0)

    def route_key(r, p2, p3, slot):
        place = {**me, d2[r]: p2, d3[r]: p3}
        expert = (place["y"] * 2 + core) * 16 + place["x"] * RING + place["z"]
        return (expert * slots + slot).astype(jnp.float32)

    sub = lax.broadcasted_iota(jnp.int32, (BLOCKS, BLOCKS * toks), 0)
    lane = lax.broadcasted_iota(jnp.int32, (BLOCKS, BLOCKS * toks), 1)
    diagonal = (sub * toks <= lane) & (lane < sub * toks + toks)

    def second_send(a, part, r, i):
        p2 = ahead(d2[r], i + 1)
        cols = pl.ds(0, widths[r]) if a else pl.ds(*part_cols(r, part))
        return send(bs[a][r].at[p2, :, :, cols], b2r[a][r].at[me[d2[r]], :, :, cols],
                    s2.at[2 * a + part, r, i], r2.at[2 * a + part, r, i], at(**{d2[r]: p2}))

    def second_parts(a):
        return range(2 - a)

    def dispatch(a, r, pair, tiles):
        unit, (slot0, count) = units[a], groups[a]

        @pl.loop(0, 2 * RING)
        def _(q):
            p2 = jnp.where(q < RING, pair[0], pair[1])
            keys = [kk[r, k] for k in range(8)]
            parts = []
            for slot in range(count):
                key = route_key(r, p2, lax.rem(q, RING), slot0 + slot)
                hit = jnp.zeros((BLOCKS, toks), jnp.float32)
                for k in range(8):
                    hit = jnp.where(keys[k] == key, 1.0, hit)
                parts.append(jnp.where(diagonal, jnp.concatenate([hit] * BLOCKS, axis=1), 0.0))
            sel[pl.ds(pl.multiple_of(q * unit, unit), unit), :] = jnp.concatenate(parts, axis=0).astype(jnp.bfloat16)

        for n, size in tiles:
            data = g[r][:, :, :, n : n + size].reshape(BLOCKS * toks, size)
            o = jnp.dot(sel[: 2 * RING * unit], data, preferred_element_type=jnp.float32).astype(jnp.bfloat16)
            o = o.reshape(2, RING, unit, size)
            for e in range(2):
                bs[a][r][pair[e], :, :, n : n + size] = o[e]

    def dispatch_first(part):
        @pl.loop(0, 2)
        def _(i):
            for r in range(3):
                dispatch(0, r, (ahead(d2[r], i + 1), ahead(d2[r], i + 3)), part_tiles(r, part))

                if part == 1:
                    @pl.when(i == 0)
                    def _():
                        second_send(0, part, r, 0).start()
                        second_send(0, part, r, 2).start()

                @pl.when(i == 1)
                def _():
                    second_send(0, part, r, 1).start()

            if part == 0:
                @pl.when(i == 0)
                def _():
                    near_step(1)
                    for r in range(3):
                        second_send(0, part, r, 0).start()
                        second_send(0, part, r, 2).start()

    def dispatch_second():
        @pl.loop(0, 2)
        def _(i):
            for r in range(3):
                dispatch(1, r, (ahead(d2[r], i + 1), ahead(d2[r], i + 3)), column_tiles(widths[r]))

    def third_source(a, r, i, p3):
        if i == 0:
            return bs[a][r].at[me[d2[r]], p3]
        return b2r[a][r].at[behind(d2[r], i), p3]

    def third_send(a, r, i, j):
        p3 = ahead(d3[r], j + 1)
        return send(third_source(a, r, i, p3), b3[a][r].at[me[d3[r]], behind(d2[r], i)],
                    s3.at[a, r, i, j], r3.at[a, r, i, j], at(**{d3[r]: p3}))

    def third_local(a, r, i):
        return local(third_source(a, r, i, me[d3[r]]), b3[a][r].at[me[d3[r]], behind(d2[r], i)], l3.at[a, r, i])

    def third_start(a, steps):
        for i in steps:
            for r in range(3):
                if i > 0:
                    for part in second_parts(a):
                        second_send(a, part, r, i - 1).wait_recv()
                for j in (1, 0, 2):
                    third_send(a, r, i, j).start()
                third_local(a, r, i).start()

    def third_finish(a):
        for i in range(RING):
            for r in range(3):
                third_local(a, r, i).wait()
                for j in range(3):
                    third_send(a, r, i, j).wait_recv()
        for r in range(3):
            for i in range(3):
                for part in second_parts(a):
                    second_send(a, part, r, i).wait_send()
                third_send(a, r, 0, i).wait_send()

    def swap_rows(a):
        unit = units[a]

        @pl.loop(0, RING)
        def _(p):
            for n, size in column_tiles(widths[1]):
                x = b3[a][1][:, p, :, n : n + size].reshape(RING * unit, size)
                y = jnp.dot(swap[a][...], x, preferred_element_type=jnp.float32)
                bs[a][1][p, :, :, n : n + size] = y.astype(jnp.bfloat16).reshape(RING, unit, size)
            for n, size in column_tiles(widths[2]):
                x = b3[a][2][p, :, :, n : n + size].reshape(RING * unit, size)
                y = jnp.dot(swap[a][...], x, preferred_element_type=jnp.float32)
                bs[a][2][:, p, :, n : n + size] = y.astype(jnp.bfloat16).reshape(RING, unit, size)

    def up(a):
        unit = units[a]
        batch = 2
        for step in range(a * h_tiles, (a + 1) * h_tiles):
            n, place = uses[step], places[step]
            for index, (needed, _, _, _) in enumerate(loads):
                if needed == step:
                    for c in w_in(index):
                        c.wait()

            @pl.loop(0, RING // batch)
            def _(q):
                p = pl.ds(q * batch, batch)
                gate = lift = None
                for r, ref in enumerate((b3[a][0], bs[a][1], bs[a][2])):
                    x = ref[p].reshape(batch * RING * unit, widths[r])
                    span = pl.ds(starts[r], widths[r])
                    gr = jnp.dot(x, wgv[place, span, :], preferred_element_type=jnp.float32)
                    ur = jnp.dot(x, wuv[place, span, :], preferred_element_type=jnp.float32)
                    gate = gr if gate is None else gate + gr
                    lift = ur if lift is None else lift + ur
                h = gate / (1.0 + jnp.exp(-gate)) * lift
                hid[a][p, :, :, n * NT : (n + 1) * NT] = h.astype(jnp.bfloat16).reshape(batch, RING, unit, NT)

            loads_after(step)

    def swap_hidden(a):
        unit = units[a]

        @pl.loop(0, RING)
        def _(p):
            x = hid[a][p].reshape(RING * unit, hidden)
            y = jnp.dot(swap[a][...], x, preferred_element_type=jnp.float32)
            hb[a][:, p] = y.astype(jnp.bfloat16).reshape(RING, unit, hidden)
            x = hid[a][:, p].reshape(RING * unit, hidden)
            y = jnp.dot(swap[a][...], x, preferred_element_type=jnp.float32)
            hc[a][p] = y.astype(jnp.bfloat16).reshape(RING, unit, hidden)

    def back_tiles(a, r, part):
        return part_tiles(r, part) if a else column_tiles(widths[r])

    def back_cols(a, r, part):
        return pl.ds(*part_cols(r, part)) if a else pl.ds(0, widths[r])

    def fourth_send(a, part, r, i):
        p3 = ahead(d3[r], i + 1)
        cols = back_cols(a, r, part)
        return send(bs[a][r].at[p3, :, :, cols], b4r[a][r].at[me[d3[r]], :, :, cols],
                    s4.at[a + part, r, i], r4.at[a + part, r, i], at(**{d3[r]: p3}))

    def down(a, part):
        unit = units[a]

        @pl.loop(0, 2)
        def _(i):
            for r, h in enumerate((hid[a], hb[a], hc[a])):
                pair = (ahead(d3[r], i + 1), ahead(d3[r], i + 3))
                x = jnp.concatenate([h[p].reshape(RING * unit, hidden) for p in pair], axis=0)
                for n, size in back_tiles(a, r, part):
                    w = wdv[:, starts[r] + n : starts[r] + n + size]
                    o = jnp.dot(x, w, preferred_element_type=jnp.float32).astype(jnp.bfloat16)
                    o = o.reshape(2, RING, unit, size)
                    for e in range(2):
                        bs[a][r][pair[e], :, :, n : n + size] = o[e]

                @pl.when(i == 0)
                def _():
                    fourth_send(a, part, r, 0).start()
                    fourth_send(a, part, r, 2).start()

                @pl.when(i == 1)
                def _():
                    fourth_send(a, part, r, 1).start()

    def fifth_source(a, part, r, i, p2):
        cols = back_cols(a, r, part)
        if i == 0:
            return bs[a][r].at[me[d3[r]], p2, :, cols]
        return b4r[a][r].at[behind(d3[r], i), p2, :, cols]

    def fifth_send(a, part, r, i, j):
        p2 = ahead(d2[r], j + 1)
        return send(fifth_source(a, part, r, i, p2), b5r[a][r].at[me[d2[r]], behind(d3[r], i), :, back_cols(a, r, part)],
                    s5.at[a + part, r, i, j], r5.at[a + part, r, i, j], at(**{d2[r]: p2}))

    def fifth_local(a, part, r, i):
        mine = me[d2[r]]
        return local(fifth_source(a, part, r, i, mine), b3[a][r].at[mine, behind(d3[r], i), :, back_cols(a, r, part)],
                     l5.at[a + part, r, i])

    def fifth_load(a, part, r, i, j):
        e2, e3, cols = behind(d2[r], j + 1), behind(d3[r], i), back_cols(a, r, part)
        return local(b5r[a][r].at[e2, e3, :, cols], b3[a][r].at[e2, e3, :, cols], ld5.at[a + part, r, i, j])

    def fifth_start(a, part, steps):
        for i in steps:
            for r in range(3):
                if i > 0:
                    fourth_send(a, part, r, i - 1).wait_recv()
                for j in (1, 0, 2):
                    fifth_send(a, part, r, i, j).start()
                fifth_local(a, part, r, i).start()

    def fifth_arrive(a, part, r):
        for i in range(RING):
            for j in range(3):
                fifth_send(a, part, r, i, j).wait_recv()
                fifth_load(a, part, r, i, j).start()

    def fifth_finish(a, part, r):
        for i in range(RING):
            fifth_local(a, part, r, i).wait()
            for j in range(3):
                fifth_load(a, part, r, i, j).wait()

    def weight_block(a, r, kb):
        if a == 0:
            return wgv.at[0, pl.ds(kb * BLOCKS * toks, BLOCKS * toks)]
        row = (2 * r + kb) * BLOCKS * toks
        return wuv.at[row // wuv.shape[1], pl.ds(row % wuv.shape[1], BLOCKS * toks)]

    def weigh(a, r):
        unit, (slot0, count) = units[a], groups[a]
        total = RING * RING * unit

        @pl.loop(0, RING * RING)
        def _(q):
            keys = [kk[r, k] for k in range(8)]
            probs = [pp[r, k] for k in range(8)]
            parts = []
            for slot in range(count):
                key = route_key(r, q // RING, lax.rem(q, RING), slot0 + slot)
                weight = jnp.zeros((BLOCKS, toks), jnp.float32)
                for k in range(8):
                    weight = jnp.where(keys[k] == key, probs[k], weight)
                parts.append(weight)
            wc[pl.ds(pl.multiple_of(q * unit, unit), unit), :] = jnp.concatenate(parts, axis=0)

        turned = wc[:total].T
        lanes = lax.broadcasted_iota(jnp.int32, (toks, NT), 1) % BLOCKS
        for kb in range(total // NT):
            part = turned[:, kb * NT : (kb + 1) * NT]
            target = weight_block(a, r, kb)
            for b in range(BLOCKS):
                target[b * toks : (b + 1) * toks, :] = jnp.where(lanes == b, part, 0.0).astype(jnp.bfloat16)

    def combine(a, r, side, tiles):
        rows = pl.ds(pl.multiple_of(side * RING * toks, RING * toks), RING * toks)
        blocks = RING * RING * units[a] // NT
        for n, size in tiles:
            x = b3[a][r][:, :, :, n : n + size].reshape(RING * RING * units[a], size)
            weights = jnp.concatenate([weight_block(a, r, kb)[rows, :] for kb in range(blocks)], axis=1)
            o = jnp.dot(weights, x, preferred_element_type=jnp.float32).reshape(RING, toks, size)
            if a:
                o = o + g[r][side, :, :, n : n + size].astype(jnp.float32)
            g[r][side, :, :, n : n + size] = o.astype(jnp.bfloat16)

    def sixth_send(r, part):
        cols = pl.ds(*part_cols(r, part))
        return send(g[r].at[mate, :, :, cols], sr[r].at[:, :, cols], s6.at[r, part], r6.at[r, part], mate_id)

    def seventh_send(r, part, i):
        p1 = ahead(d1[r], i + 1)
        n, size = part_cols(r, part)
        return send(g[r].at[core, p1, :, pl.ds(n, size)], rr[r].at[i, :, pl.ds(n, size)],
                    s7.at[r, part, i], r7.at[r, part, i], at(**{d1[r]: p1}))

    dispatch_first(0)
    relay_step(1)
    dispatch_first(1)
    third_start(0, (0,))
    dispatch_second()
    third_start(0, (1, 2, 3))
    for r in range(3):
        for i in (0, 2, 1):
            second_send(1, 0, r, i).start()
    third_start(1, (0,))
    third_finish(0)
    swap_rows(0)
    up(0)
    swap_hidden(0)
    wd_in.wait()
    third_start(1, (1, 2, 3))
    down(0, 0)
    fifth_start(0, 0, (0,))
    third_finish(1)
    swap_rows(1)
    up(1)
    swap_hidden(1)
    fifth_start(0, 0, (1, 2, 3))
    for part in range(2):
        down(1, part)
        fifth_start(1, part, (0,))
    for r in range(3):
        for part in range(2):
            for k in range(5):
                mate_send(part, r, k).wait_send()
            for w in range(2):
                relay_send(part, r, w).wait_send()
    for r in range(3):
        weigh(1, r)
    for r in range(3):
        weigh(0, r)
        fifth_arrive(0, 0, r)
        fifth_finish(0, 0, r)
        combine(0, r, mate, column_tiles(widths[r]))
        combine(0, r, core, column_tiles(widths[r]))
    for part in range(2):
        fifth_start(1, part, (1, 2, 3))

    for part in range(2):
        for r in range(3):
            fifth_arrive(1, part, r)
        for r in range(3):
            fifth_finish(1, part, r)
            combine(1, r, mate, part_tiles(r, part))
            sixth_send(r, part).start()
        for r in range(3):
            combine(1, r, core, part_tiles(r, part))
        for r in range(3):
            sixth_send(r, part).wait_recv()
            n, size = part_cols(r, part)

            for i in range(3):
                p1 = ahead(d1[r], i + 1)
                total = g[r][core, p1, :, n : n + size].astype(jnp.float32) + sr[r][p1, :, n : n + size].astype(jnp.float32)
                g[r][core, p1, :, n : n + size] = total.astype(jnp.bfloat16)
                seventh_send(r, part, i).start()

    for part in range(2):
        for r in range(3):
            n, size = part_cols(r, part)
            mine = me[d1[r]]
            total = g[r][core, mine, :, n : n + size].astype(jnp.float32) + sr[r][mine, :, n : n + size].astype(jnp.float32)
            for i in range(3):
                seventh_send(r, part, i).wait_recv()
                total = total + rr[r][i, :, n : n + size].astype(jnp.float32)
            out[:, starts[r] + n : starts[r] + n + size] = total.astype(jnp.bfloat16)

    for r in range(3):
        for part in range(2):
            sixth_send(r, part).wait_send()
            for i in range(3):
                seventh_send(r, part, i).wait_send()
    for r in range(3):
        for i in range(3):
            route_send(r, i).wait_send()
        for i in range(4):
            route_mate(r, i).wait_send()
        for part in range(2):
            for w in range(2):
                near_send(part, r, w).wait_send()
    for r in range(3):
        for a in range(2):
            for i in range(RING):
                for j in range(3):
                    if i > 0:
                        third_send(a, r, i, j).wait_send()
                    for part in range(1 + a):
                        fifth_send(a, part, r, i, j).wait_send()
            for i in range(3):
                for part in range(1 + a):
                    fourth_send(a, part, r, i).wait_send()


def shards(tokens, expert_ids, slot_positions, gate_probs, w_gate, w_up, w_down):
    toks, width = tokens.shape
    experts = lax.axis_size(("grp", "slc"))
    slots = max(2, toks * expert_ids.shape[1] * 5 // (4 * experts))
    lead = 2 * ((slots + 2) // 4)
    groups = ((0, lead), (lead, slots - lead))
    units = [count * BLOCKS for _, count in groups]
    hidden = w_gate.shape[2]
    widths, starts = chunk_widths(width)
    swaps = [jnp.asarray(swap_matrix(count), jnp.bfloat16) for _, count in groups]
    bf, f32 = jnp.bfloat16, jnp.float32
    hbm = [jax.ShapeDtypeStruct((RING, RING, u, w), bf) for _ in range(3) for u in units for w in widths]
    dma = pltpu.SemaphoreType.DMA
    vmem = pltpu.VMEM
    scratch = (
        [vmem((2, RING, toks, w), bf) for w in widths]
        + [vmem((RING, RING, u, w), bf) for _ in range(2) for u in units for w in widths]
        + [vmem((RING, toks, w), bf) for w in widths]
        + [vmem((3, toks, w), bf) for w in widths]
        + [vmem((RING, RING, u, hidden), bf) for _ in range(3) for u in units]
        + [
            vmem((16, toks), f32),
            vmem((3, 2, RING, 16, toks), f32),
            vmem((3, 8, BLOCKS, toks), f32),
            vmem((3, 8, BLOCKS, toks), f32),
            vmem((2 * RING * units[0], BLOCKS * toks), bf),
            vmem((RING * RING * units[0], toks), f32),
            vmem((2, width, NT), bf),
            vmem((2, width, NT), bf),
            vmem((hidden, width), bf),
        ]
        + [dma((16,)), dma((3,))]
        + [dma((2, 3, 2))] * 4
        + [dma((3, 3))] * 2
        + [dma((2, 3, 5))] * 2
        + [dma((3, 4))] * 2
        + [dma((3, 3, 3))] * 2
        + [dma((2, 3, 4, 3))] * 2
        + [dma((2, 3, 4))]
        + [dma((3, 3, 3))] * 2
        + [dma((3, 3, 4, 3))] * 2
        + [dma((3, 3, 4)), dma((3, 3, 4, 3))]
        + [dma((3, 2))] * 2
        + [dma((3, 2, 3))] * 2
    )
    any_spec = pl.BlockSpec(memory_space=pl.ANY)
    vmem_spec = pl.BlockSpec(memory_space=pltpu.VMEM)
    results = pl.pallas_call(
        functools.partial(kernel, groups, widths, starts),
        out_shape=[jax.ShapeDtypeStruct((toks, width), bf)] + hbm,
        in_specs=[any_spec] + [vmem_spec] * 5 + [any_spec] * 3,
        out_specs=[vmem_spec] + [any_spec] * len(hbm),
        scratch_shapes=scratch,
        compiler_params=pltpu.CompilerParams(
            collective_id=0, has_side_effects=True, vmem_limit_bytes=65000 * 1024
        ),
    )(tokens, expert_ids.T, slot_positions.T, gate_probs.T, *swaps,
      w_gate.reshape(width, hidden), w_up.reshape(width, hidden), w_down.reshape(hidden, width))
    return results[0]


def solution(mesh):
    row = P(("grp", "slc"), None)
    cube = P(("grp", "slc"), None, None)
    return jax.shard_map(
        shards, mesh=mesh, in_specs=(row, row, row, row, cube, cube, cube), out_specs=row, check_vma=False
    )
```

```python
import functools

import jax
import jax.numpy as jnp
import numpy as np
from jax import lax
from jax.experimental import pallas as pl
from jax.experimental.pallas import tpu as pltpu
from jax.sharding import PartitionSpec as P

MESH = pl.DeviceIdType.MESH
RING = 4
BLOCKS = 2 * RING
NT = 256
ORDERS = (("y", "x", "z"), ("x", "z", "y"), ("z", "y", "x"))


def chunk_widths(width):
    tiles = width // 128
    widths = [128 * ((tiles + 2 - r) // 3) for r in range(3)]
    return widths, [0, widths[0], widths[0] + widths[1]]


def swap_matrix(slots):
    unit = slots * BLOCKS
    q = np.arange(RING * unit)
    a, slot, c, b = q // unit, q % unit // BLOCKS, q % BLOCKS // RING, q % RING
    target = b * unit + slot * BLOCKS + c * RING + a
    return (np.arange(RING * unit)[:, None] == target[None, :]).astype(np.float32)


def column_tiles(width):
    return [(n, min(NT, width - n)) for n in range(0, width, NT)]


def kernel(groups, widths, starts, tok, ids, places_in, probs_in, swap0, swap1, wg, wu, wd, out, *refs):
    refs = list(refs)

    def take(count):
        taken, refs[:count] = refs[:count], []
        return taken

    b2r, b4r, b5r = ([take(3), take(3)] for _ in range(3))
    g = take(3)
    bs, b3 = ([take(3), take(3)] for _ in range(2))
    sr, rr = take(3), take(3)
    hid, hb, hc = (take(2) for _ in range(3))
    meta, km, kk, pp, sel, wc, wgv, wuv, wdv = take(9)
    wsem, own_sem, s1, r1, sb, rb, sm1, rm1, sf, rf, smf, rmf = take(12)
    s2, r2, s3, r3, l3, s4, r4, s5, r5, l5, ld5, s6, r6, s7, r7 = take(15)
    swap = (swap0, swap1)
    units = [count * BLOCKS for _, count in groups]
    slots = sum(count for _, count in groups)
    toks = tok.shape[0]
    hidden = wdv.shape[0]
    grp, slc = lax.axis_index("grp"), lax.axis_index("slc")
    me = {"y": grp // 2, "c": lax.rem(grp, 2), "x": slc // RING, "z": lax.rem(slc, RING)}
    core = me["c"]
    mate = 1 - core

    def at(**changes):
        coords = {**me, **changes}
        return (coords["y"] * 2 + coords["c"], coords["x"] * RING + coords["z"])

    def ahead(d, k):
        return lax.rem(me[d] + k, RING)

    def behind(d, k):
        return lax.rem(me[d] + RING - k, RING)

    def send(src, dst, ssem, rsem, where):
        return pltpu.make_async_remote_copy(
            src_ref=src, dst_ref=dst, send_sem=ssem, recv_sem=rsem, device_id=where, device_id_type=MESH
        )

    def local(src, dst, sem):
        return pltpu.make_async_copy(src, dst, sem)

    mate_id = at(c=mate)
    d1 = [o[0] for o in ORDERS]
    d2 = [o[1] for o in ORDERS]
    d3 = [o[2] for o in ORDERS]
    h_tiles = hidden // NT
    uses = list(range(h_tiles)) + [(n + 1) % h_tiles for n in range(h_tiles)]
    places, loads = [], []
    held = {}
    for step, n in enumerate(uses):
        if n not in held:
            if len(held) < 2:
                place, after = len(held), -1
            else:
                oldest = uses[step - 2]
                place, after = held.pop(oldest), step - 2
            held[n] = place
            loads.append((step, n, place, after))
        places.append(held[n])

    def w_in(index):
        _, n, place, _ = loads[index]
        cols = pl.ds(n * NT, NT)
        return (local(wg.at[:, cols], wgv.at[place], wsem.at[2 * index]),
                local(wu.at[:, cols], wuv.at[place], wsem.at[2 * index + 1]))

    def loads_after(step):
        for index, (_, _, _, after) in enumerate(loads):
            if after == step:
                for c in w_in(index):
                    c.start()

    chosen = jnp.where(places_in[...] < slots, ids[...] * slots + places_in[...], -1)
    meta[0:8] = chosen.astype(jnp.float32)
    meta[8:16] = probs_in[...]
    loads_after(-1)
    wd_in = local(wd, wdv, wsem.at[2 * len(loads)])
    wd_in.start()

    def tok_cols(r):
        return tok.at[:, pl.ds(starts[r], widths[r])]

    own_in = [local(tok_cols(r), g[r].at[core, me[d1[r]]], own_sem.at[r]) for r in range(3)]
    for c in own_in:
        c.start()

    barrier = pltpu.get_barrier_semaphore()
    greet = [mate_id] + [at(**{d: ahead(d, k)}) for d in ("x", "y", "z") for k in (1, 2, 3)]
    for where in greet:
        pl.semaphore_signal(barrier, inc=1, device_id=where, device_id_type=MESH)
    pl.semaphore_wait(barrier, len(greet))

    half = toks // 2
    lower, upper = pl.ds(0, half), pl.ds(half, half)
    ways = ((1, (lower, upper)), (3, (upper, lower)))
    first, pending, relays = [], [], []

    def to_mate(r, source, rows, index):
        ref = g[r].at[core, source, rows]
        c = send(ref, ref, sf.at[r, index], rf.at[r, index], mate_id)
        c.start()
        pending.append((r, c))

    routes = []
    for r in range(3):
        mine = me[d1[r]]
        for i in range(3):
            c = send(meta, km.at[r, core, mine], sm1.at[r, i], rm1.at[r, i], at(**{d1[r]: ahead(d1[r], i + 1)}))
            c.start()
            routes.append((r, i, c))
        c = send(meta, km.at[r, core, mine], smf.at[r, 0], rmf.at[r, 0], mate_id)
        c.start()
        pending.append((r, c))
    near = {}
    for h in range(2):
        for r in range(3):
            mine = me[d1[r]]
            for w, (way, halves) in enumerate(ways):
                src = tok.at[halves[h], pl.ds(starts[r], widths[r])]
                c = send(src, g[r].at[core, mine, halves[h]], s1.at[r, w, h], r1.at[r, w, h], at(**{d1[r]: ahead(d1[r], way)}))
                c.start()
                near[r, w, h] = c
    for r in range(3):
        mine = me[d1[r]]
        c = send(tok_cols(r), g[r].at[core, mine], sf.at[r, 0], rf.at[r, 0], mate_id)
        c.start()
        pending.append((r, c))
        km[r, core, mine] = meta[...]
    for h in range(2):
        for r in range(3):
            for w, (way, halves) in enumerate(ways):
                source = behind(d1[r], way)
                near[r, w, h].wait_recv()
                if h == 0:
                    ref = g[r].at[core, source, halves[0]]
                    c = send(ref, ref, sb.at[r, w], rb.at[r, w], at(**{d1[r]: ahead(d1[r], way)}))
                    c.start()
                    relays.append((r, w, c))
                to_mate(r, source, halves[h], 1 + 2 * w + h)
        if h == 0:
            for r, i, c in routes:
                source = behind(d1[r], i + 1)
                c.wait_recv()
                c = send(km.at[r, core, source], km.at[r, core, source], smf.at[r, i + 1], rmf.at[r, i + 1], mate_id)
                c.start()
                pending.append((r, c))
    for r, w, c in relays:
        c.wait_recv()
        to_mate(r, behind(d1[r], 2), ways[w][1][0], 5 + w)
    first = [c for _, _, c in routes] + list(near.values())
    for c in own_in:
        c.wait()
    for _, c in pending:
        c.wait_recv()
    for r in range(3):
        for k in range(8):
            kk[r, k] = jnp.concatenate([km[r, b // RING, b % RING, k : k + 1] for b in range(BLOCKS)], axis=0)
            pp[r, k] = jnp.concatenate([km[r, b // RING, b % RING, 8 + k : 9 + k] for b in range(BLOCKS)], axis=0)

    def route_key(r, p2, p3, slot):
        place = {**me, d2[r]: p2, d3[r]: p3}
        expert = (place["y"] * 2 + core) * 16 + place["x"] * RING + place["z"]
        return (expert * slots + slot).astype(jnp.float32)

    sub = lax.broadcasted_iota(jnp.int32, (BLOCKS, BLOCKS * toks), 0)
    lane = lax.broadcasted_iota(jnp.int32, (BLOCKS, BLOCKS * toks), 1)
    diagonal = (sub * toks <= lane) & (lane < sub * toks + toks)

    def second_send(a, r, i):
        p2 = ahead(d2[r], i + 1)
        return send(bs[a][r].at[p2], b2r[a][r].at[me[d2[r]]], s2.at[a, r, i], r2.at[a, r, i], at(**{d2[r]: p2}))

    def dispatch(a, r, pair):
        unit, (slot0, count) = units[a], groups[a]

        @pl.loop(0, 2 * RING)
        def _(q):
            p2 = jnp.where(q < RING, pair[0], pair[1])
            keys = [kk[r, k] for k in range(8)]
            parts = []
            for slot in range(count):
                key = route_key(r, p2, lax.rem(q, RING), slot0 + slot)
                hit = jnp.zeros((BLOCKS, toks), jnp.float32)
                for k in range(8):
                    hit = jnp.where(keys[k] == key, 1.0, hit)
                parts.append(jnp.where(diagonal, jnp.concatenate([hit] * BLOCKS, axis=1), 0.0))
            sel[pl.ds(pl.multiple_of(q * unit, unit), unit), :] = jnp.concatenate(parts, axis=0).astype(jnp.bfloat16)

        for n, size in column_tiles(widths[r]):
            data = g[r][:, :, :, n : n + size].reshape(BLOCKS * toks, size)
            o = jnp.dot(sel[: 2 * RING * unit], data, preferred_element_type=jnp.float32).astype(jnp.bfloat16)
            o = o.reshape(2, RING, unit, size)
            for e in range(2):
                bs[a][r][pair[e], :, :, n : n + size] = o[e]

    def dispatch_all(a, sending):
        @pl.loop(0, 2)
        def _(i):
            for r in range(3):
                dispatch(a, r, (ahead(d2[r], i + 1), ahead(d2[r], i + 3)))
                if sending:
                    @pl.when(i == 0)
                    def _():
                        second_send(a, r, 0).start()
                        second_send(a, r, 2).start()

                    @pl.when(i == 1)
                    def _():
                        second_send(a, r, 1).start()

    def third_source(a, r, i, p3):
        if i == 0:
            return bs[a][r].at[me[d2[r]], p3]
        return b2r[a][r].at[behind(d2[r], i), p3]

    def third_send(a, r, i, j):
        p3 = ahead(d3[r], j + 1)
        return send(third_source(a, r, i, p3), b3[a][r].at[me[d3[r]], behind(d2[r], i)],
                    s3.at[a, r, i, j], r3.at[a, r, i, j], at(**{d3[r]: p3}))

    def third_local(a, r, i):
        return local(third_source(a, r, i, me[d3[r]]), b3[a][r].at[me[d3[r]], behind(d2[r], i)], l3.at[a, r, i])

    def third_start(a, steps):
        for i in steps:
            for r in range(3):
                if i > 0:
                    second_send(a, r, i - 1).wait_recv()
                for j in (1, 0, 2):
                    third_send(a, r, i, j).start()
                third_local(a, r, i).start()

    def third_finish(a):
        for i in range(RING):
            for r in range(3):
                third_local(a, r, i).wait()
                for j in range(3):
                    third_send(a, r, i, j).wait_recv()
        for r in range(3):
            for i in range(3):
                second_send(a, r, i).wait_send()
                third_send(a, r, 0, i).wait_send()

    def swap_rows(a):
        unit = units[a]

        @pl.loop(0, RING)
        def _(p):
            for n, size in column_tiles(widths[1]):
                x = b3[a][1][:, p, :, n : n + size].reshape(RING * unit, size)
                y = jnp.dot(swap[a][...], x, preferred_element_type=jnp.float32)
                bs[a][1][p, :, :, n : n + size] = y.astype(jnp.bfloat16).reshape(RING, unit, size)
            for n, size in column_tiles(widths[2]):
                x = b3[a][2][p, :, :, n : n + size].reshape(RING * unit, size)
                y = jnp.dot(swap[a][...], x, preferred_element_type=jnp.float32)
                bs[a][2][:, p, :, n : n + size] = y.astype(jnp.bfloat16).reshape(RING, unit, size)

    def up(a):
        unit = units[a]
        batch = 2
        for step in range(a * h_tiles, (a + 1) * h_tiles):
            n, place = uses[step], places[step]
            for index, (needed, _, _, _) in enumerate(loads):
                if needed == step:
                    for c in w_in(index):
                        c.wait()

            @pl.loop(0, RING // batch)
            def _(q):
                p = pl.ds(q * batch, batch)
                gate = lift = None
                for r, ref in enumerate((b3[a][0], bs[a][1], bs[a][2])):
                    x = ref[p].reshape(batch * RING * unit, widths[r])
                    span = pl.ds(starts[r], widths[r])
                    gr = jnp.dot(x, wgv[place, span, :], preferred_element_type=jnp.float32)
                    ur = jnp.dot(x, wuv[place, span, :], preferred_element_type=jnp.float32)
                    gate = gr if gate is None else gate + gr
                    lift = ur if lift is None else lift + ur
                h = gate / (1.0 + jnp.exp(-gate)) * lift
                hid[a][p, :, :, n * NT : (n + 1) * NT] = h.astype(jnp.bfloat16).reshape(batch, RING, unit, NT)

            loads_after(step)

    def swap_hidden(a):
        unit = units[a]

        @pl.loop(0, RING)
        def _(p):
            x = hid[a][p].reshape(RING * unit, hidden)
            y = jnp.dot(swap[a][...], x, preferred_element_type=jnp.float32)
            hb[a][:, p] = y.astype(jnp.bfloat16).reshape(RING, unit, hidden)
            x = hid[a][:, p].reshape(RING * unit, hidden)
            y = jnp.dot(swap[a][...], x, preferred_element_type=jnp.float32)
            hc[a][p] = y.astype(jnp.bfloat16).reshape(RING, unit, hidden)

    def part_tiles(r, part):
        tiles = column_tiles(widths[r])
        middle = (len(tiles) + 1) // 2
        return tiles[:middle] if part == 0 else tiles[middle:]

    def part_cols(r, part):
        tiles = part_tiles(r, part)
        return tiles[0][0], tiles[-1][0] + tiles[-1][1] - tiles[0][0]

    def back_tiles(a, r, part):
        return part_tiles(r, part) if a else column_tiles(widths[r])

    def back_cols(a, r, part):
        return pl.ds(*part_cols(r, part)) if a else pl.ds(0, widths[r])

    def fourth_send(a, part, r, i):
        p3 = ahead(d3[r], i + 1)
        cols = back_cols(a, r, part)
        return send(bs[a][r].at[p3, :, :, cols], b4r[a][r].at[me[d3[r]], :, :, cols],
                    s4.at[a + part, r, i], r4.at[a + part, r, i], at(**{d3[r]: p3}))

    def down(a, part):
        unit = units[a]

        @pl.loop(0, 2)
        def _(i):
            for r, h in enumerate((hid[a], hb[a], hc[a])):
                pair = (ahead(d3[r], i + 1), ahead(d3[r], i + 3))
                x = jnp.concatenate([h[p].reshape(RING * unit, hidden) for p in pair], axis=0)
                for n, size in back_tiles(a, r, part):
                    w = wdv[:, starts[r] + n : starts[r] + n + size]
                    o = jnp.dot(x, w, preferred_element_type=jnp.float32).astype(jnp.bfloat16)
                    o = o.reshape(2, RING, unit, size)
                    for e in range(2):
                        bs[a][r][pair[e], :, :, n : n + size] = o[e]

                @pl.when(i == 0)
                def _():
                    fourth_send(a, part, r, 0).start()
                    fourth_send(a, part, r, 2).start()

                @pl.when(i == 1)
                def _():
                    fourth_send(a, part, r, 1).start()

    def fifth_source(a, part, r, i, p2):
        cols = back_cols(a, r, part)
        if i == 0:
            return bs[a][r].at[me[d3[r]], p2, :, cols]
        return b4r[a][r].at[behind(d3[r], i), p2, :, cols]

    def fifth_send(a, part, r, i, j):
        p2 = ahead(d2[r], j + 1)
        return send(fifth_source(a, part, r, i, p2), b5r[a][r].at[me[d2[r]], behind(d3[r], i), :, back_cols(a, r, part)],
                    s5.at[a + part, r, i, j], r5.at[a + part, r, i, j], at(**{d2[r]: p2}))

    def fifth_local(a, part, r, i):
        mine = me[d2[r]]
        return local(fifth_source(a, part, r, i, mine), b3[a][r].at[mine, behind(d3[r], i), :, back_cols(a, r, part)],
                     l5.at[a + part, r, i])

    def fifth_load(a, part, r, i, j):
        e2, e3, cols = behind(d2[r], j + 1), behind(d3[r], i), back_cols(a, r, part)
        return local(b5r[a][r].at[e2, e3, :, cols], b3[a][r].at[e2, e3, :, cols], ld5.at[a + part, r, i, j])

    def fifth_start(a, part, steps):
        for i in steps:
            for r in range(3):
                if i > 0:
                    fourth_send(a, part, r, i - 1).wait_recv()
                for j in (1, 0, 2):
                    fifth_send(a, part, r, i, j).start()
                fifth_local(a, part, r, i).start()

    def fifth_arrive(a, part, r):
        for i in range(RING):
            for j in range(3):
                fifth_send(a, part, r, i, j).wait_recv()
                fifth_load(a, part, r, i, j).start()

    def fifth_finish(a, part, r):
        for i in range(RING):
            fifth_local(a, part, r, i).wait()
            for j in range(3):
                fifth_load(a, part, r, i, j).wait()

    def weight_block(a, r, kb):
        if a == 0:
            return wgv.at[0, pl.ds(kb * BLOCKS * toks, BLOCKS * toks)]
        row = (2 * r + kb) * BLOCKS * toks
        return wuv.at[row // wuv.shape[1], pl.ds(row % wuv.shape[1], BLOCKS * toks)]

    def weigh(a, r):
        unit, (slot0, count) = units[a], groups[a]
        total = RING * RING * unit

        @pl.loop(0, RING * RING)
        def _(q):
            keys = [kk[r, k] for k in range(8)]
            probs = [pp[r, k] for k in range(8)]
            parts = []
            for slot in range(count):
                key = route_key(r, q // RING, lax.rem(q, RING), slot0 + slot)
                weight = jnp.zeros((BLOCKS, toks), jnp.float32)
                for k in range(8):
                    weight = jnp.where(keys[k] == key, probs[k], weight)
                parts.append(weight)
            wc[pl.ds(pl.multiple_of(q * unit, unit), unit), :] = jnp.concatenate(parts, axis=0)

        turned = wc[:total].T
        lanes = lax.broadcasted_iota(jnp.int32, (toks, NT), 1) % BLOCKS
        for kb in range(total // NT):
            part = turned[:, kb * NT : (kb + 1) * NT]
            target = weight_block(a, r, kb)
            for b in range(BLOCKS):
                target[b * toks : (b + 1) * toks, :] = jnp.where(lanes == b, part, 0.0).astype(jnp.bfloat16)

    def combine(a, r, side, tiles):
        rows = pl.ds(pl.multiple_of(side * RING * toks, RING * toks), RING * toks)
        blocks = RING * RING * units[a] // NT
        for n, size in tiles:
            x = b3[a][r][:, :, :, n : n + size].reshape(RING * RING * units[a], size)
            weights = jnp.concatenate([weight_block(a, r, kb)[rows, :] for kb in range(blocks)], axis=1)
            o = jnp.dot(weights, x, preferred_element_type=jnp.float32).reshape(RING, toks, size)
            if a:
                o = o + g[r][side, :, :, n : n + size].astype(jnp.float32)
            g[r][side, :, :, n : n + size] = o.astype(jnp.bfloat16)

    def sixth_send(r, part):
        cols = pl.ds(*part_cols(r, part))
        return send(g[r].at[mate, :, :, cols], sr[r].at[:, :, cols], s6.at[r, part], r6.at[r, part], mate_id)

    def seventh_send(r, part, i):
        p1 = ahead(d1[r], i + 1)
        n, size = part_cols(r, part)
        return send(g[r].at[core, p1, :, pl.ds(n, size)], rr[r].at[i, :, pl.ds(n, size)],
                    s7.at[r, part, i], r7.at[r, part, i], at(**{d1[r]: p1}))

    dispatch_all(0, True)
    third_start(0, (0,))
    dispatch_all(1, False)
    third_start(0, (1, 2, 3))
    for r in range(3):
        for i in (0, 2, 1):
            second_send(1, r, i).start()
    third_start(1, (0,))
    third_finish(0)
    swap_rows(0)
    up(0)
    swap_hidden(0)
    wd_in.wait()
    third_start(1, (1, 2, 3))
    down(0, 0)
    fifth_start(0, 0, (0,))
    third_finish(1)
    swap_rows(1)
    up(1)
    swap_hidden(1)
    fifth_start(0, 0, (1, 2, 3))
    for part in range(2):
        down(1, part)
        fifth_start(1, part, (0,))
    for c in [c for _, c in pending] + [c for _, _, c in relays]:
        c.wait_send()
    for r in range(3):
        weigh(1, r)
    for r in range(3):
        weigh(0, r)
        fifth_arrive(0, 0, r)
        fifth_finish(0, 0, r)
        combine(0, r, mate, column_tiles(widths[r]))
        combine(0, r, core, column_tiles(widths[r]))
    for part in range(2):
        fifth_start(1, part, (1, 2, 3))

    for part in range(2):
        for r in range(3):
            fifth_arrive(1, part, r)
        for r in range(3):
            fifth_finish(1, part, r)
            combine(1, r, mate, part_tiles(r, part))
            sixth_send(r, part).start()
        for r in range(3):
            combine(1, r, core, part_tiles(r, part))
        for r in range(3):
            sixth_send(r, part).wait_recv()
            n, size = part_cols(r, part)

            for i in range(3):
                p1 = ahead(d1[r], i + 1)
                total = g[r][core, p1, :, n : n + size].astype(jnp.float32) + sr[r][p1, :, n : n + size].astype(jnp.float32)
                g[r][core, p1, :, n : n + size] = total.astype(jnp.bfloat16)
                seventh_send(r, part, i).start()

    for part in range(2):
        for r in range(3):
            n, size = part_cols(r, part)
            mine = me[d1[r]]
            total = g[r][core, mine, :, n : n + size].astype(jnp.float32) + sr[r][mine, :, n : n + size].astype(jnp.float32)
            for i in range(3):
                seventh_send(r, part, i).wait_recv()
                total = total + rr[r][i, :, n : n + size].astype(jnp.float32)
            out[:, starts[r] + n : starts[r] + n + size] = total.astype(jnp.bfloat16)

    for r in range(3):
        for part in range(2):
            sixth_send(r, part).wait_send()
            for i in range(3):
                seventh_send(r, part, i).wait_send()
    for c in first:
        c.wait_send()
    for r in range(3):
        for a in range(2):
            for i in range(RING):
                for j in range(3):
                    if i > 0:
                        third_send(a, r, i, j).wait_send()
                    for part in range(1 + a):
                        fifth_send(a, part, r, i, j).wait_send()
            for i in range(3):
                for part in range(1 + a):
                    fourth_send(a, part, r, i).wait_send()


def shards(tokens, expert_ids, slot_positions, gate_probs, w_gate, w_up, w_down):
    toks, width = tokens.shape
    experts = lax.axis_size(("grp", "slc"))
    slots = max(2, toks * expert_ids.shape[1] * 5 // (4 * experts))
    lead = 2 * ((slots + 2) // 4)
    groups = ((0, lead), (lead, slots - lead))
    units = [count * BLOCKS for _, count in groups]
    hidden = w_gate.shape[2]
    widths, starts = chunk_widths(width)
    swaps = [jnp.asarray(swap_matrix(count), jnp.bfloat16) for _, count in groups]
    bf, f32 = jnp.bfloat16, jnp.float32
    hbm = [jax.ShapeDtypeStruct((RING, RING, u, w), bf) for _ in range(3) for u in units for w in widths]
    dma = pltpu.SemaphoreType.DMA
    vmem = pltpu.VMEM
    scratch = (
        [vmem((2, RING, toks, w), bf) for w in widths]
        + [vmem((RING, RING, u, w), bf) for _ in range(2) for u in units for w in widths]
        + [vmem((RING, toks, w), bf) for w in widths]
        + [vmem((3, toks, w), bf) for w in widths]
        + [vmem((RING, RING, u, hidden), bf) for _ in range(3) for u in units]
        + [
            vmem((16, toks), f32),
            vmem((3, 2, RING, 16, toks), f32),
            vmem((3, 8, BLOCKS, toks), f32),
            vmem((3, 8, BLOCKS, toks), f32),
            vmem((2 * RING * units[0], BLOCKS * toks), bf),
            vmem((RING * RING * units[0], toks), f32),
            vmem((2, width, NT), bf),
            vmem((2, width, NT), bf),
            vmem((hidden, width), bf),
        ]
        + [dma((16,)), dma((3,))]
        + [dma((3, 2, 2))] * 2
        + [dma((3, 2))] * 2
        + [dma((3, 3))] * 2
        + [dma((3, 7))] * 2
        + [dma((3, 4))] * 2
        + [dma((2, 3, 3))] * 2
        + [dma((2, 3, 4, 3))] * 2
        + [dma((2, 3, 4))]
        + [dma((3, 3, 3))] * 2
        + [dma((3, 3, 4, 3))] * 2
        + [dma((3, 3, 4)), dma((3, 3, 4, 3))]
        + [dma((3, 2))] * 2
        + [dma((3, 2, 3))] * 2
    )
    any_spec = pl.BlockSpec(memory_space=pl.ANY)
    vmem_spec = pl.BlockSpec(memory_space=pltpu.VMEM)
    results = pl.pallas_call(
        functools.partial(kernel, groups, widths, starts),
        out_shape=[jax.ShapeDtypeStruct((toks, width), bf)] + hbm,
        in_specs=[any_spec] + [vmem_spec] * 5 + [any_spec] * 3,
        out_specs=[vmem_spec] + [any_spec] * len(hbm),
        scratch_shapes=scratch,
        compiler_params=pltpu.CompilerParams(
            collective_id=0, has_side_effects=True, vmem_limit_bytes=65000 * 1024
        ),
    )(tokens, expert_ids.T, slot_positions.T, gate_probs.T, *swaps,
      w_gate.reshape(width, hidden), w_up.reshape(width, hidden), w_down.reshape(hidden, width))
    return results[0]


def solution(mesh):
    row = P(("grp", "slc"), None)
    cube = P(("grp", "slc"), None, None)
    return jax.shard_map(
        shards, mesh=mesh, in_specs=(row, row, row, row, cube, cube, cube), out_specs=row, check_vma=False
    )
```
